256 devices in a mesh: row: 32 (over y_lo, z, core), col: 8 (over x, y_hi).
Axes of the slice: x: 4, y: 4 (y_hi: 2, y_lo: 2; y = y_hi * 2 + y_lo), z: 8, core: 2. Of those that a mesh axis runs over, the one named last changes fastest.
Arguments:
- momentum: bfloat16 [5376, 9216], P('row', 'col'), may hold values from -3 to 3
Outputs:
- update: bfloat16 [5376, 9216], P('row', 'col')
The draws below stay inside these ranges and needn't reach their ends.
All inputs are finite; a program needn't handle non-finite values.
Results may differ from the reference program's by a relative error of at most 0.0041.
Values may be sent and summed in bfloat16 or wider, within the bound.
A program may use at most 64 MiB of HBM per device.

```python
import jax
import jax.numpy as jnp

HEIGHT = 5376
BREADTH = 9216


def block_levels(own_key, dims, split, low, largest):
    def one(position, blocks):
        draws = jax.random.uniform(jax.random.fold_in(jax.random.fold_in(own_key, 6), position), (blocks,), jnp.float32, low / len(split), largest / len(split))
        return jnp.repeat(jnp.exp(draws), dims[position] // blocks).reshape((-1,) + (1,) * (len(dims) - position - 1))

    loudness = one(*split[0])
    for cut in split[1:]:
        loudness = loudness * one(*cut)
    return loudness


def scatter_about(rng, shape, deviation, most, shards=(), dtype=jnp.bfloat16):
    array = jax.random.normal(rng, shape, jnp.float32) * deviation
    if len(shards) > 0:
        array = block_levels(rng, shape, shards, -0.22, 0.18) * array
    return jnp.clip(array, min=-most, max=most).astype(dtype)


def setup_inputs(seed: int = 0) -> dict:
    seeds = jax.random.split(jax.random.key(seed), 2)
    return {
        "momentum": scatter_about(seeds[0], (HEIGHT, BREADTH), 0.55, 3.0, ((0, 32), (1, 8))),
    }


coef_a = 3.4445
coef_b = -4.7750
coef_c = 2.0315


def reference(momentum):
    gram_f32 = jnp.dot(momentum, momentum.T, preferred_element_type=jnp.float32) * (1.0 / BREADTH)
    gram_bf = gram_f32.astype(jnp.bfloat16)
    first = jnp.dot(gram_bf, momentum, preferred_element_type=jnp.float32)
    first_bf = first.astype(jnp.bfloat16)
    second = jnp.dot(gram_bf, first_bf, preferred_element_type=jnp.float32)
    result = coef_a * momentum.astype(jnp.float32) + coef_b * first + coef_c * second
    return result.astype(jnp.bfloat16)
```

```python
import jax
import jax.numpy as jnp
from jax import lax
from jax.experimental import pallas as pl
from jax.experimental.pallas import tpu as pltpu
from jax.sharding import PartitionSpec as P

BREADTH = 9216
MESH = pl.DeviceIdType.MESH
F32 = jnp.float32
BF16 = jnp.bfloat16

coef_a = 3.4445
coef_b = -4.775
coef_c = 2.0315

ROWS = 168
PAD = 192
WIDTH = 384
CHUNKS = 3
ZS, YS, XS = 8, 4, 4
PIECE = PAD // XS


def place(x, y, z, c):
    return (lax.rem(y, 2) * 16 + z * 2 + c, x * 2 + y // 2)


def padded(block):
    tail = jnp.zeros((PAD - ROWS, WIDTH), F32)
    return jnp.concatenate([block.astype(F32), tail], axis=0).astype(BF16)


def kernel(
    m_ref, o_ref,
    x_blk, f_blk, mz_blk, x_flat, f_flat, mz_flat,
    ex, er, gsum, gs, gr, gg, gt,
    own, first, s1, r1, s2, r2, outp, outr,
    in_s, in_r, xz_s, xz_r, fz_s, fz_r, mz_s, mz_r,
    ex_s, ex_r, gr_s, gr_r, gx_s, gx_r, gc_s, gc_r,
    r1_s, r1_r, r2_s, r2_r, out_s, out_r,
):
    row, col = lax.axis_index("row"), lax.axis_index("col")
    x, y_hi = col // 2, lax.rem(col, 2)
    y_lo, z, c = row // 16, lax.rem(row // 2, ZS), lax.rem(row, 2)
    y = y_hi * 2 + y_lo

    def at_z(d):
        return place(x, y, lax.rem(z + d + ZS, ZS), c)

    def at_y(d):
        return place(x, lax.rem(y + d + YS, YS), z, c)

    def at_x(d):
        return place(lax.rem(x + d + XS, XS), y, z, c)

    other_core = place(x, y, z, 1 - c)
    partner = place(x, c * 2 + y_lo, z, y_hi)
    stays = c == y_hi

    sends = []

    def copy(src, dst, send, recv, to):
        return pltpu.make_async_remote_copy(
            src_ref=src, dst_ref=dst, send_sem=send, recv_sem=recv,
            device_id=to, device_id_type=MESH,
        )

    def go(cp):
        cp.start()
        sends.append(cp)

    barrier = pltpu.get_barrier_semaphore()
    peers = [at_z(1), at_z(-1), other_core]
    peers += [at_y(d) for d in (1, 2, 3)] + [at_x(d) for d in (1, 2, 3)]
    for peer in peers:
        pl.semaphore_signal(barrier, inc=1, device_id=peer, device_id_type=MESH)

    @pl.when(jnp.logical_not(stays))
    def _():
        pl.semaphore_signal(barrier, inc=1, device_id=partner, device_id_type=MESH)
        pl.semaphore_wait(barrier, len(peers) + 1)

    @pl.when(stays)
    def _():
        pl.semaphore_wait(barrier, len(peers))

    def cols(q):
        return pl.ds(q * WIDTH, WIDTH)

    def move_in(q):
        return copy(m_ref.at[:, cols(q)], x_blk.at[0, q], in_s.at[q], in_r.at[q], partner)

    @pl.when(stays)
    def _():
        for q in range(CHUNKS):
            x_blk[0, q] = m_ref[:, cols(q)]

    @pl.when(jnp.logical_not(stays))
    def _():
        for q in range(CHUNKS):
            move_in(q).start()

    def z_copy(blk, ss, rs, dst, q):
        if dst > 4 or (dst == 4 and q < 2):
            src, to = (dst + 1) % ZS, at_z(1)
        else:
            src, to = dst - 1, at_z(-1)
        return copy(blk.at[src, q], blk.at[dst, q], ss.at[dst, q], rs.at[dst, q], to)

    def x_copy(dst, q):
        return z_copy(x_blk, xz_s, xz_r, dst, q)

    def f_copy(dst, q):
        return z_copy(f_blk, fz_s, fz_r, dst, q)

    def mz_copy(j, q):
        return copy(
            x_blk.at[0, q], mz_blk.at[j - 1, q], mz_s.at[j - 1, q], mz_r.at[j - 1, q], at_y(-j)
        )

    def relay(make, s, q):
        for slot, nxt, far in ((ZS - s, ZS - s - 1, q < 2), (s, s + 1, q >= 2)):
            make(slot, q).wait_recv()
            if s < 3 or far:
                go(make(nxt, q))

    for q in range(CHUNKS):

        @pl.when(jnp.logical_not(stays))
        def _():
            move_in(q).wait_recv()

        go(x_copy(7, q))
        go(x_copy(1, q))
        for j in (1, 3, 2):
            go(mz_copy(j, q))

    def flatten(blk, flat, i, q):
        flat[q, i * PAD:(i + 1) * PAD, :] = padded(blk[i, q])

    def slot_of(t, core):
        return 4 * core if t == 3 else (t + 1) + core * (6 - 2 * t)

    def span(i, start=0, size=PAD):
        return pl.ds(pl.multiple_of(i * PAD + start, 16), size)

    def piece(p):
        return pl.ds(pl.multiple_of(p * PIECE, 16), PIECE)

    def gram_part(i):
        total = None
        for q in range(CHUNKS):
            part = lax.dot_general(
                x_flat[q, span(i), :], mz_flat[q], (((1,), (1,)), ((), ())),
                preferred_element_type=F32,
            )
            total = part if total is None else total + part
        return total * (1.0 / BREADTH)

    def ex_copy(t):
        return copy(ex.at[t], er.at[t], ex_s.at[t], ex_r.at[t], other_core)

    def gr_copy(t, d):
        p = lax.rem(x + d, XS)
        return copy(
            gs.at[t, piece(p)], gr.at[t, d - 1], gr_s.at[t, d - 1], gr_r.at[t, d - 1], at_x(d)
        )

    def gx_copy(t, d, p):
        where = gg.at[span(slot_of(t, c), p * PIECE, PIECE)]
        return copy(where, where, gx_s.at[t, d - 1], gx_r.at[t, d - 1], at_x(d))

    def gc_copy(t, core):
        where = gg.at[span(slot_of(t, core))]
        return copy(where, where, gc_s.at[t], gc_r.at[t], other_core)

    def stage_a(t):
        ex[t] = gram_part(slot_of(t, 1 - c))
        go(ex_copy(t))
        gsum[t] = gram_part(slot_of(t, c))

    def stage_b(t):
        ex_copy(t).wait_recv()
        total = gsum[t] + er[t]
        gsum[t] = total
        gs[t] = total.astype(BF16)
        for d in (1, 3, 2):
            go(gr_copy(t, d))

    def stage_c(t):
        for d in (1, 3, 2):
            gr_copy(t, d).wait_recv()
        total = gsum[t, piece(x), :]
        for d in range(3):
            total = total + gr[t, d].astype(F32)
        gg[span(slot_of(t, c), x * PIECE, PIECE), :] = total.astype(BF16)
        for d in (1, 3, 2):
            go(gx_copy(t, d, x))

    def stage_d(t):
        for d in (1, 3, 2):
            gx_copy(t, d, lax.rem(x - d + XS, XS)).wait_recv()
        go(gc_copy(t, c))

    def stage_e(t):
        gc_copy(t, 1 - c).wait_recv()

    def relay_all(s):
        for q in range(CHUNKS):
            relay(x_copy, s, q)
        for q in range(CHUNKS):
            flatten(x_blk, x_flat, s, q)
            flatten(x_blk, x_flat, ZS - s, q)

    for q in range(CHUNKS):
        flatten(x_blk, x_flat, 0, q)
    relay_all(1)
    relay_all(2)
    for q in range(CHUNKS):
        mz_flat[q, 0:PAD, :] = padded(x_blk[0, q])
        for j in (1, 3, 2):
            mz_copy(j, q).wait_recv()
            mz_flat[q, j * PAD:(j + 1) * PAD, :] = padded(mz_blk[j - 1, q])
    stage_a(0)
    stage_a(1)
    stage_b(0)
    stage_b(1)
    stage_c(0)
    relay_all(3)
    stage_a(2)
    stage_c(1)
    stage_b(2)
    stage_d(0)
    for q in range(CHUNKS):
        x_copy(4, q).wait_recv()
        flatten(x_blk, x_flat, 4, q)
    stage_a(3)
    stage_d(1)
    stage_b(3)
    stage_c(2)
    stage_c(3)
    stage_d(2)
    stage_d(3)
    for t in range(4):
        stage_e(t)

    for a in range(ZS * PAD // 128):
        gt[:, a * 128:(a + 1) * 128] = gg[a * 128:(a + 1) * 128, :].T

    def times_gram(flat, q, s, r, ss, rs):
        part = jnp.dot(gt[...], flat[q], preferred_element_type=F32)
        for j in (2, 1, 3):
            s[j - 1, q] = part[j * PAD:j * PAD + ROWS].astype(BF16)
            go(y_copy(s, r, ss, rs, j, q))
        own[q] = part[:ROWS]

    def y_copy(s, r, ss, rs, j, q):
        return copy(s.at[j - 1, q], r.at[j - 1, q], ss.at[j - 1, q], rs.at[j - 1, q], at_y(j))

    def summed(s, r, ss, rs, q):
        total = own[q]
        for j in (1, 3, 2):
            y_copy(s, r, ss, rs, j, q).wait_recv()
            total = total + r[j - 1, q].astype(F32)
        return total

    one = (s1, r1, r1_s, r1_r)
    two = (s2, r2, r2_s, r2_r)

    for q in range(CHUNKS):
        times_gram(x_flat, q, *one)

    def start_first(q):
        total = summed(*one, q)
        first[q] = total
        f_blk[0, q] = total.astype(BF16)
        go(f_copy(7, q))
        go(f_copy(1, q))

    def finish_ring(q):
        f_copy(4, q).wait_recv()
        for i in range(ZS):
            flatten(f_blk, f_flat, i, q)
        times_gram(f_flat, q, *two)

    def move_out(q):
        return copy(outp.at[q], outr.at[q], out_s.at[q], out_r.at[q], partner)

    def finish(q):
        second = summed(*two, q)
        result = coef_a * x_blk[0, q].astype(F32) + coef_b * first[q] + coef_c * second
        result = result.astype(BF16)

        @pl.when(stays)
        def _():
            o_ref[:, cols(q)] = result

        @pl.when(jnp.logical_not(stays))
        def _():
            outp[q] = result
            move_out(q).start()

    start_first(0)
    relay(f_copy, 1, 0)
    start_first(1)
    relay(f_copy, 2, 0)
    relay(f_copy, 1, 1)
    start_first(2)
    relay(f_copy, 3, 0)
    relay(f_copy, 2, 1)
    relay(f_copy, 1, 2)
    finish_ring(0)
    relay(f_copy, 3, 1)
    relay(f_copy, 2, 2)
    finish_ring(1)
    relay(f_copy, 3, 2)
    finish(0)
    finish_ring(2)
    finish(1)
    finish(2)

    @pl.when(jnp.logical_not(stays))
    def _():
        for q in range(CHUNKS):
            move_out(q).wait_recv()
            o_ref[:, cols(q)] = outr[q]
        for q in range(CHUNKS):
            move_in(q).wait_send()
            move_out(q).wait_send()

    for cp in sends:
        cp.wait_send()


def shards(momentum):
    vm, dma = pltpu.VMEM, pltpu.SemaphoreType.DMA
    blk = (CHUNKS, ROWS, WIDTH)
    scratch = [
        vm((ZS,) + blk, BF16), vm((ZS,) + blk, BF16), vm((3,) + blk, BF16),
        vm((CHUNKS, ZS * PAD, WIDTH), BF16), vm((CHUNKS, ZS * PAD, WIDTH), BF16),
        vm((CHUNKS, YS * PAD, WIDTH), BF16),
        vm((4, PAD, YS * PAD), F32), vm((4, PAD, YS * PAD), F32), vm((4, PAD, YS * PAD), F32),
        vm((4, PAD, YS * PAD), BF16), vm((4, 3, PIECE, YS * PAD), BF16),
        vm((ZS * PAD, YS * PAD), BF16), vm((YS * PAD, ZS * PAD), BF16),
        vm(blk, F32), vm(blk, F32),
        vm((3,) + blk, BF16), vm((3,) + blk, BF16), vm((3,) + blk, BF16), vm((3,) + blk, BF16),
        vm(blk, BF16), vm(blk, BF16),
    ]
    q = CHUNKS
    for shape in ((q,), (ZS, q), (ZS, q), (3, q), (4,), (4, 3), (4, 3), (4,), (3, q), (3, q), (q,)):
        scratch += [dma(shape), dma(shape)]
    return pl.pallas_call(
        kernel,
        out_shape=jax.ShapeDtypeStruct((ROWS, CHUNKS * WIDTH), BF16),
        in_specs=[pl.BlockSpec(memory_space=pltpu.VMEM)],
        out_specs=pl.BlockSpec(memory_space=pltpu.VMEM),
        scratch_shapes=scratch,
        compiler_params=pltpu.CompilerParams(
            collective_id=0, has_side_effects=True, vmem_limit_bytes=56 * 1024 * 1024
        ),
        name="newton_schulz",
    )(momentum)


def solution(mesh):
    in_specs = (P("row", "col"),)
    out_specs = P("row", "col")
    return jax.shard_map(shards, mesh=mesh, in_specs=in_specs, out_specs=out_specs, check_vma=False)
```

```python
import jax
import jax.numpy as jnp
from jax import lax
from jax.experimental import pallas as pl
from jax.experimental.pallas import tpu as pltpu
from jax.sharding import PartitionSpec as P

BREADTH = 9216
MESH = pl.DeviceIdType.MESH
F32 = jnp.float32
BF16 = jnp.bfloat16

coef_a = 3.4445
coef_b = -4.775
coef_c = 2.0315

ROWS, COLS = 168, 1152
PAD = 192
ZS, YS, XS = 8, 4, 4
PIECE = PAD // XS
LANE = 128
RING_X = (1, 2, 2, 2, 2)
RING_F = (1, 1, 1, 1, 2, 2, 1)
RIGHT_X = (1, 2)
RIGHT_F = (0, 1, 2, 3)
STEPS = (
    "p0", "p1", "p2", "p3", "p4", "p5", "p6", "s0", "s1", "r01", "s2", "r11", "s3", "r02", "r21",
    "r12", "r31", "s4", "r03", "r22", "r13", "r32", "s5", "r41", "s6", "h0", "h1", "r04", "g0",
    "r23", "r14", "g1", "h2", "h3", "r33", "r51", "r42", "h4", "r61", "r24", "g2", "r34", "g3",
    "h5", "r52", "r43", "h6", "r44", "r62", "g4", "f0", "f1", "r53", "r54", "g5", "f2", "r63",
    "r64", "g6", "f3", "f4", "f5", "f6",
)
SLOTS = (1, 7, 2, 6, 3, 5, 0, 4)


def chunks(widths):
    spans, start = [], 0
    for w in widths:
        spans.append(pl.ds(start * LANE, w * LANE))
        start += w
    return spans


def place(x, y, z, c):
    return (lax.rem(y, 2) * 16 + z * 2 + c, x * 2 + y // 2)


def flatten(src, dst, start, cols):
    for l in range(cols.start, cols.start + cols.size, LANE):
        tail = jnp.zeros((PAD - ROWS, LANE), F32)
        block = jnp.concatenate([src[:, l:l + LANE].astype(F32), tail], axis=0)
        dst[start:start + PAD, l:l + LANE] = block.astype(BF16)


def kernel(
    m_ref, o_ref,
    mz_blk, x_blk, f_blk, mz_flat, x_flat, f_flat,
    ex, er, gsum, gs, gr, gg, gt,
    acc, own, first, first_in, s1, r1, s2, r2,
    mz_s, mz_r, xz_s, xz_r, fz_s, fz_r,
    ex_s, ex_r, gr_s, gr_r, gx_s, gx_r, gc_s, gc_r,
    r1_s, r1_r, r2_s, r2_r, out_s, out_r,
):
    row, col = lax.axis_index("row"), lax.axis_index("col")
    x, y_hi = col // 2, lax.rem(col, 2)
    y_lo, z, c = row // 16, lax.rem(row // 2, ZS), lax.rem(row, 2)
    y = y_hi * 2 + y_lo

    def at_z(d):
        return place(x, y, lax.rem(z + d + ZS, ZS), c)

    def at_y(d):
        return place(x, lax.rem(y + d + YS, YS), z, c)

    def at_x(d):
        return place(lax.rem(x + d + XS, XS), y, z, c)

    other_core = place(x, y, z, 1 - c)
    home = c * 2 + y_lo

    def taker(j):
        return place(x, lax.rem(home - j + YS, YS), z, y_hi)

    partner = taker(0)

    def owner(j):
        to = lax.rem(y + j, YS)
        return place(x, c * 2 + lax.rem(to, 2), z, to // 2)

    stays = c == y_hi
    moves = jnp.logical_not(stays)

    sends = []

    def copy(src, dst, send, recv, to):
        return pltpu.make_async_remote_copy(
            src_ref=src, dst_ref=dst, send_sem=send, recv_sem=recv,
            device_id=to, device_id_type=MESH,
        )

    def go(cp):
        cp.start()
        sends.append(cp)

    barrier = pltpu.get_barrier_semaphore()

    def greet(peer):
        pl.semaphore_signal(barrier, inc=1, device_id=peer, device_id_type=MESH)

    for peer in (
        [at_z(1), at_z(-1), other_core]
        + [at_y(d) for d in (1, 2, 3)] + [at_x(d) for d in (1, 2, 3)]
        + [taker(j) for j in (1, 2, 3)] + [owner(j) for j in (1, 2, 3)]
    ):
        greet(peer)

    @pl.when(moves)
    def _():
        greet(partner)
        pl.semaphore_wait(barrier, 16)

    @pl.when(stays)
    def _():
        pl.semaphore_wait(barrier, 15)

    span_x, span_f = chunks(RING_X), chunks(RING_F)

    def mz_copy(j, q):
        where = mz_blk.at[j, :, span_x[q]]
        return copy(m_ref.at[:, span_x[q]], where, mz_s.at[j, q], mz_r.at[j, q], taker(j))

    @pl.when(stays)
    def _():
        mz_blk[0] = m_ref[...]

    @pl.when(moves)
    def _():
        for q in range(len(span_x)):
            mz_copy(0, q).start()

    def z_copy(own_blk, blk, spans, right, ss, rs, dst, q):
        if dst > 4 or (dst == 4 and q in right):
            src, to = (dst + 1) % ZS, at_z(1)
        else:
            src, to = dst - 1, at_z(-1)
        src_ref = own_blk.at[:, spans[q]] if src == 0 else blk.at[src - 1, :, spans[q]]
        return copy(src_ref, blk.at[dst - 1, :, spans[q]], ss.at[dst, q], rs.at[dst, q], to)

    def x_copy(dst, q):
        return z_copy(mz_blk.at[0], x_blk, span_x, RIGHT_X, xz_s, xz_r, dst, q)

    def f_copy(dst, q):
        return z_copy(f_blk.at[7], f_blk, span_f, RIGHT_F, fz_s, fz_r, dst, q)

    def relay(make, right, s, q):
        if s == 4:
            make(4, q).wait_recv()
            return
        for slot, nxt, far in ((ZS - s, ZS - s - 1, q in right), (s, s + 1, q not in right)):
            make(slot, q).wait_recv()
            if s < 3 or far:
                go(make(nxt, q))

    for q in range(len(span_x)):

        @pl.when(moves)
        def _():
            mz_copy(0, q).wait_recv()

        go(x_copy(7, q))
        go(x_copy(1, q))

    whole = pl.ds(0, COLS)

    def span(t, core, start=0, size=PAD):
        return pl.ds(pl.multiple_of((2 * t + core) * PAD + start, 16), size)

    def piece(p):
        return pl.ds(pl.multiple_of(p * PIECE, 16), PIECE)

    def ex_copy(t):
        return copy(ex.at[t], er.at[t], ex_s.at[t], ex_r.at[t], other_core)

    def gr_copy(t, d):
        p = lax.rem(x + d, XS)
        return copy(
            gs.at[t, piece(p)], gr.at[t, d - 1], gr_s.at[t, d - 1], gr_r.at[t, d - 1], at_x(d)
        )

    def gx_copy(t, d, p):
        where = gg.at[span(t, c, p * PIECE, PIECE)]
        return copy(where, where, gx_s.at[t, d - 1], gx_r.at[t, d - 1], at_x(d))

    def gc_copy(t, core):
        where = gg.at[span(t, core)]
        return copy(where, where, gc_s.at[t], gc_r.at[t], other_core)

    def flatten_x(*slots):
        for slot in slots:
            src = mz_blk.at[0] if slot == 0 else x_blk.at[slot - 1]
            flatten(src, x_flat, SLOTS.index(slot) * PAD, whole)

    def relay_one(s, q):
        relay(x_copy, RIGHT_X, s, q)

    def stage_a(t):
        part = lax.dot_general(
            x_flat[2 * t * PAD:2 * (t + 1) * PAD, :], mz_flat[...], (((1,), (1,)), ((), ())),
            preferred_element_type=F32,
        )
        part = part * (1.0 / BREADTH)
        ex[t] = jnp.where(c == 0, part[PAD:], part[:PAD])
        go(ex_copy(t))
        gsum[t] = jnp.where(c == 0, part[:PAD], part[PAD:])

    def stage_b(t):
        ex_copy(t).wait_recv()
        total = gsum[t] + er[t]
        gsum[t] = total
        gs[t] = total.astype(BF16)
        for d in (1, 3, 2):
            go(gr_copy(t, d))

    def stage_c(t):
        for d in (1, 3, 2):
            gr_copy(t, d).wait_recv()
        total = gsum[t, piece(x), :]
        for d in range(3):
            total = total + gr[t, d].astype(F32)
        gg[span(t, c, x * PIECE, PIECE), :] = total.astype(BF16)
        for d in (1, 3, 2):
            go(gx_copy(t, d, x))

    def stage_d(t):
        for d in (1, 3, 2):
            gx_copy(t, d, lax.rem(x - d + XS, XS)).wait_recv()
        go(gc_copy(t, c))

    def stage_e(t):
        gc_copy(t, 1 - c).wait_recv()
        for a in range(2 * PAD * t, 2 * PAD * (t + 1), LANE):
            gt[:, a:a + LANE] = gg[a:a + LANE, :].T

    def relay_one(s, q):
        relay(x_copy, RIGHT_X, s, q)

    def part_of(block):
        part = lax.dot_general(
            x_flat[block * PAD:(block + 1) * PAD, :], mz_flat[...], (((1,), (1,)), ((), ())),
            preferred_element_type=F32,
        )
        part = part * (1.0 / BREADTH)

        @pl.when(c == block % 2)
        def _():
            gsum[block // 2] = part

        @pl.when(c != block % 2)
        def _():
            ex[block // 2] = part
            ex_copy(block // 2).start()

    def on_core(core, stage, t):
        @pl.when(c == core)
        def _():
            before = len(sends)
            stage(t)
            del sends[before:]

    nx = len(span_x)
    flatten_x(0)
    flatten(mz_blk.at[0], mz_flat, 0, whole)
    for q in range(nx):
        relay_one(1, q)
        if q == 1:
            for i in range(nx):
                for j in (1, 3, 2):
                    go(mz_copy(j, i))
    flatten_x(1, 7)
    relay_one(2, 0)
    relay_one(2, 1)
    for j in (1, 3, 2):
        for q in range(nx):
            mz_copy(j, q).wait_recv()
        flatten(mz_blk.at[j], mz_flat, j * PAD, whole)
    stage_a(0)
    sends += [ex_copy(3), gc_copy(3, c)]
    sends += [gr_copy(3, d) for d in (1, 2, 3)] + [gx_copy(3, d, x) for d in (1, 2, 3)]
    part_of(6)
    relay_one(2, 2)
    stage_b(0)
    relay_one(2, 3)
    on_core(0, stage_b, 3)
    relay_one(2, 4)
    flatten_x(2, 6)
    stage_a(1)
    relay_one(3, 0)
    stage_b(1)
    relay_one(3, 1)
    stage_c(0)
    relay_one(3, 2)
    on_core(0, stage_c, 3)
    relay_one(3, 3)
    stage_c(1)
    relay_one(3, 4)
    flatten_x(3, 5)
    stage_a(2)
    stage_d(0)
    on_core(0, stage_d, 3)
    stage_b(2)
    stage_d(1)
    for q in range(nx):
        relay_one(4, q)
    flatten_x(4)
    part_of(7)
    stage_c(2)
    stage_e(0)
    on_core(1, stage_b, 3)
    stage_e(1)
    stage_d(2)
    on_core(1, stage_c, 3)
    stage_e(2)
    early = 6 * PAD
    acc[...] = jnp.dot(gt[:, :early], x_flat[:early, :], preferred_element_type=F32)
    on_core(1, stage_d, 3)
    stage_e(3)

    def y_copy(j, q):
        where = (j, slice(None), span_f[q])
        return copy(s1.at[where], r1.at[where], r1_s.at[j, q], r1_r.at[j, q], at_y(j))

    def last_copy(j, q):
        where = (j, slice(None), span_f[q])
        return copy(s2.at[where], r2.at[where], r2_s.at[j, q], r2_r.at[j, q], owner(j))

    def start_ring(q):
        cols = span_f[q]
        total = own[:, cols]
        for j in (1, 3, 2):
            y_copy(j, q).wait_recv()
            total = total + r1[j, :, cols].astype(F32)
        first[:, cols] = total
        f_blk[7, :, cols] = total.astype(BF16)
        go(f_copy(7, q))
        go(f_copy(1, q))
        flatten(f_blk.at[7], f_flat, SLOTS.index(0) * PAD, cols)

    def first_copy(q):
        where = (slice(None), span_f[q])
        return copy(first.at[where], first_in.at[where], out_s.at[q], out_r.at[q], partner)

    def hand_over(q):
        @pl.when(moves)
        def _():
            first_copy(q).start()

    def finish(q):
        cols = span_f[q]
        for j in (1, 3, 2):
            last_copy(j, q).wait_recv()

        @pl.when(moves)
        def _():
            first_copy(q).wait_recv()
            last_copy(0, q).wait_recv()

        @pl.when(stays)
        def _():
            first_in[:, cols] = first[:, cols]
            r2[0, :, cols] = s2[0, :, cols]

        second = r2[0, :, cols].astype(F32)
        for j in (1, 3, 2):
            second = second + r2[j, :, cols].astype(F32)
        result = coef_a * m_ref[:, cols].astype(F32) + coef_b * first_in[:, cols] + coef_c * second
        o_ref[:, cols] = result.astype(BF16)

    count = len(span_f)

    def product(q):
        cols = span_f[q]
        part = acc[:, cols] + jnp.dot(gt[:, early:], x_flat[early:, cols], preferred_element_type=F32)
        for j in (2, 1, 3):
            s1[j, :, cols] = part[j * PAD:j * PAD + ROWS].astype(BF16)
            go(y_copy(j, q))
        own[:, cols] = part[:ROWS]

    def second_product(q):
        cols = span_f[q]
        part = jnp.dot(gt[...], f_flat[:, cols], preferred_element_type=F32)
        for j in (2, 1, 3, 0):
            s2[j, :, cols] = part[j * PAD:j * PAD + ROWS].astype(BF16)
            if j > 0:
                go(last_copy(j, q))

        @pl.when(moves)
        def _():
            last_copy(0, q).start()

    def arrive(q, s):
        relay(f_copy, RIGHT_F, s, q)
        for slot in {1: (1, 7), 2: (2, 6), 3: (3, 5), 4: (4,)}[s]:
            flatten(f_blk.at[slot - 1], f_flat, SLOTS.index(slot) * PAD, span_f[q])

    act = {
        "p": product, "s": start_ring, "h": hand_over, "r": arrive, "g": second_product,
        "f": finish,
    }
    for step in STEPS:
        act[step[0]](*map(int, step[1:]))
        if step[0] == "r":
            for cp in sends[:5]:
                cp.wait_send()
            del sends[:5]

    @pl.when(moves)
    def _():
        for q in range(nx):
            mz_copy(0, q).wait_send()
        for q in range(count):
            first_copy(q).wait_send()
            last_copy(0, q).wait_send()

    for cp in sends:
        cp.wait_send()


def shards(momentum):
    vm, dma = pltpu.VMEM, pltpu.SemaphoreType.DMA
    blk = (ROWS, COLS)
    lanes = YS * PAD
    scratch = [
        vm((YS,) + blk, BF16), vm((ZS - 1,) + blk, BF16), vm((ZS,) + blk, BF16),
        vm((lanes, COLS), BF16), vm((ZS * PAD, COLS), BF16), vm((ZS * PAD, COLS), BF16),
        vm((4, PAD, lanes), F32), vm((4, PAD, lanes), F32), vm((4, PAD, lanes), F32),
        vm((4, PAD, lanes), BF16), vm((4, 3, PIECE, lanes), BF16),
        vm((ZS * PAD, lanes), BF16), vm((lanes, ZS * PAD), BF16),
        vm((lanes, COLS), F32), vm(blk, F32), vm(blk, F32), vm(blk, F32),
        vm((YS,) + blk, BF16), vm((YS,) + blk, BF16), vm((YS,) + blk, BF16), vm((YS,) + blk, BF16),
    ]
    nx, nf = len(RING_X), len(RING_F)
    for shape in (
        (YS, nx), (ZS, nx), (ZS, nf), (4,), (4, 3), (4, 3), (4,), (YS, nf), (YS, nf), (nf,)
    ):
        scratch += [dma(shape), dma(shape)]
    return pl.pallas_call(
        kernel,
        out_shape=jax.ShapeDtypeStruct(blk, BF16),
        in_specs=[pl.BlockSpec(memory_space=pltpu.VMEM)],
        out_specs=pl.BlockSpec(memory_space=pltpu.VMEM),
        scratch_shapes=scratch,
        compiler_params=pltpu.CompilerParams(
            collective_id=0, has_side_effects=True, vmem_limit_bytes=56 * 1024 * 1024
        ),
        name="newton_schulz",
    )(momentum)


def solution(mesh):
    in_specs = (P("row", "col"),)
    out_specs = P("row", "col")
    return jax.shard_map(shards, mesh=mesh, in_specs=in_specs, out_specs=out_specs, check_vma=False)
```

```python
import jax
import jax.numpy as jnp
from jax import lax
from jax.experimental import pallas as pl
from jax.experimental.pallas import tpu as pltpu
from jax.sharding import PartitionSpec as P

BREADTH = 9216
MESH = pl.DeviceIdType.MESH
F32 = jnp.float32
BF16 = jnp.bfloat16

coef_a = 3.4445
coef_b = -4.775
coef_c = 2.0315

ROWS, COLS = 168, 1152
ZS, YS, XS = 8, 4, 4
LANE = 128
RING_X = (1, 2, 2, 2, 2)
RING_F = (1, 1, 1, 1, 2, 2, 1)
RIGHT_X = (1, 2)
RIGHT_F = (0, 1, 2, 3)
STEPS = (
    "p0", "p1", "p2", "p3", "p4", "p5", "p6", "s0", "s1", "r01", "s2", "r11", "s3", "r02", "r21",
    "r12", "r31", "s4", "r03", "r22", "r13", "r32", "s5", "r41", "s6", "h0", "h1", "r04", "g0",
    "r23", "r14", "g1", "h2", "h3", "r33", "r51", "r42", "h4", "r61", "r24", "g2", "r34", "g3",
    "h5", "r52", "r43", "h6", "r44", "r62", "g4", "f0", "f1", "r53", "r54", "g5", "f2", "r63",
    "r64", "g6", "f3", "f4", "f5", "f6",
)
UNITS = (((0, 1, 7), 0, 512), ((2, 6), 512, 384), ((3, 5), 896, 384), ((4,), 1280, 256))
DEPTH = 1536
HEIGHT = YS * ROWS
TILE = 2 * LANE
TILES = DEPTH // TILE


def chunks(widths):
    spans, start = [], 0
    for w in widths:
        spans.append(pl.ds(start * LANE, w * LANE))
        start += w
    return spans


def place(x, y, z, c):
    return (lax.rem(y, 2) * 16 + z * 2 + c, x * 2 + y // 2)


def flatten(blocks, dst, start, rows, cols):
    empty = rows - ROWS * len(blocks)
    for l in range(cols.start, cols.start + cols.size, LANE):
        parts = [blk[:, l:l + LANE].astype(F32) for blk in blocks]
        if empty:
            parts.append(jnp.zeros((empty, LANE), F32))
        stacked = parts[0] if len(parts) == 1 else jnp.concatenate(parts, axis=0)
        dst[start:start + rows, l:l + LANE] = stacked.astype(BF16)


def kernel(
    m_ref, o_ref,
    mz_blk, x_blk, f_blk, mz_flat, x_flat, f_flat,
    ex, er, gsum, gs, gr, gg, gt,
    acc, own, first, first_in, s1, r1, s2, r2,
    mz_s, mz_r, xz_s, xz_r, fz_s, fz_r,
    ex_s, ex_r, gr_s, gr_r, gx_s, gx_r, gc_s, gc_r,
    r1_s, r1_r, r2_s, r2_r, out_s, out_r,
):
    row, col = lax.axis_index("row"), lax.axis_index("col")
    x, y_hi = col // 2, lax.rem(col, 2)
    y_lo, z, c = row // 16, lax.rem(row // 2, ZS), lax.rem(row, 2)
    y = y_hi * 2 + y_lo

    def at_z(d):
        return place(x, y, lax.rem(z + d + ZS, ZS), c)

    def at_y(d):
        return place(x, lax.rem(y + d + YS, YS), z, c)

    def at_x(d):
        return place(lax.rem(x + d + XS, XS), y, z, c)

    other_core = place(x, y, z, 1 - c)
    home = c * 2 + y_lo

    def taker(j):
        return place(x, lax.rem(home - j + YS, YS), z, y_hi)

    partner = taker(0)

    def owner(j):
        to = lax.rem(y + j, YS)
        return place(x, c * 2 + lax.rem(to, 2), z, to // 2)

    stays = c == y_hi
    moves = jnp.logical_not(stays)

    sends = []

    def copy(src, dst, send, recv, to):
        return pltpu.make_async_remote_copy(
            src_ref=src, dst_ref=dst, send_sem=send, recv_sem=recv,
            device_id=to, device_id_type=MESH,
        )

    def go(cp):
        cp.start()
        sends.append(cp)

    barrier = pltpu.get_barrier_semaphore()

    def greet(peer):
        pl.semaphore_signal(barrier, inc=1, device_id=peer, device_id_type=MESH)

    for peer in (
        [at_z(1), at_z(-1), other_core]
        + [at_y(d) for d in (1, 2, 3)] + [at_x(d) for d in (1, 2, 3)]
        + [taker(j) for j in (1, 2, 3)] + [owner(j) for j in (1, 2, 3)]
    ):
        greet(peer)

    @pl.when(moves)
    def _():
        greet(partner)
        pl.semaphore_wait(barrier, 16)

    @pl.when(stays)
    def _():
        pl.semaphore_wait(barrier, 15)

    span_x, span_f = chunks(RING_X), chunks(RING_F)

    def mz_copy(j, q):
        where = mz_blk.at[j, :, span_x[q]]
        return copy(m_ref.at[:, span_x[q]], where, mz_s.at[j, q], mz_r.at[j, q], taker(j))

    @pl.when(stays)
    def _():
        mz_blk[0] = m_ref[...]

    @pl.when(moves)
    def _():
        for q in range(len(span_x)):
            mz_copy(0, q).start()

    def z_copy(own_blk, blk, spans, right, ss, rs, dst, q):
        if dst > 4 or (dst == 4 and q in right):
            src, to = (dst + 1) % ZS, at_z(1)
        else:
            src, to = dst - 1, at_z(-1)
        src_ref = own_blk.at[:, spans[q]] if src == 0 else blk.at[src - 1, :, spans[q]]
        return copy(src_ref, blk.at[dst - 1, :, spans[q]], ss.at[dst, q], rs.at[dst, q], to)

    def x_copy(dst, q):
        return z_copy(mz_blk.at[0], x_blk, span_x, RIGHT_X, xz_s, xz_r, dst, q)

    def f_copy(dst, q):
        return z_copy(f_blk.at[7], f_blk, span_f, RIGHT_F, fz_s, fz_r, dst, q)

    def relay(make, right, s, q):
        if s == 4:
            make(4, q).wait_recv()
            return
        for slot, nxt, far in ((ZS - s, ZS - s - 1, q in right), (s, s + 1, q not in right)):
            make(slot, q).wait_recv()
            if s < 3 or far:
                go(make(nxt, q))

    for q in range(len(span_x)):

        @pl.when(moves)
        def _():
            mz_copy(0, q).wait_recv()

        go(x_copy(7, q))
        go(x_copy(1, q))

    whole = pl.ds(0, COLS)

    def lanes(u, core):
        return pl.ds(pl.multiple_of((2 * u + core) * LANE, LANE), LANE)

    def ex_copy(u):
        return copy(ex.at[u], er.at[u], ex_s.at[u], ex_r.at[u], other_core)

    def gr_copy(u, d):
        p = lax.rem(x + d, XS)
        return copy(
            gs.at[u, p], gr.at[u, d - 1], gr_s.at[u, d - 1], gr_r.at[u, d - 1], at_x(d)
        )

    def gx_copy(u, d, p):
        where = gg.at[p, :, lanes(u, c)]
        return copy(where, where, gx_s.at[u, d - 1], gx_r.at[u, d - 1], at_x(d))

    def gc_copy(u, core):
        where = gg.at[:, :, lanes(u, core)]
        return copy(where, where, gc_s.at[u], gc_r.at[u], other_core)

    def flatten_x(s):
        slots, start, rows = UNITS[s - 1]
        blocks = [mz_blk.at[0] if k == 0 else x_blk.at[k - 1] for k in slots]
        flatten(blocks, x_flat, start, rows, whole)

    def relay_one(s, q):
        relay(x_copy, RIGHT_X, s, q)

    def stage_a(u):
        part = lax.dot_general(
            mz_flat[...], x_flat[u * TILE:(u + 1) * TILE, :], (((1,), (1,)), ((), ())),
            preferred_element_type=F32,
        )
        part = part * (1.0 / BREADTH)
        ex[u] = jnp.where(c == 0, part[:, LANE:], part[:, :LANE])
        go(ex_copy(u))
        gsum[u] = jnp.where(c == 0, part[:, :LANE], part[:, LANE:])

    def stage_b(u):
        ex_copy(u).wait_recv()
        total = gsum[u] + er[u]
        gsum[u] = total
        for p in range(XS):
            gs[u, p] = total[p * ROWS:(p + 1) * ROWS].astype(BF16)
        for d in (1, 3, 2):
            go(gr_copy(u, d))

    def stage_c(u):
        for d in (1, 3, 2):
            gr_copy(u, d).wait_recv()
        total = gsum[u, pl.ds(pl.multiple_of(x * ROWS, 8), ROWS), :]
        for d in range(3):
            total = total + gr[u, d].astype(F32)
        gg[x, :, lanes(u, c)] = total.astype(BF16)
        for d in (1, 3, 2):
            go(gx_copy(u, d, x))

    def stage_d(u):
        for d in (1, 3, 2):
            gx_copy(u, d, lax.rem(x - d + XS, XS)).wait_recv()
        go(gc_copy(u, c))

    def stage_e(u):
        gc_copy(u, 1 - c).wait_recv()
        flatten([gg.at[p] for p in range(XS)], gt, 0, HEIGHT, pl.ds(u * TILE, TILE))

    nx = len(span_x)
    for q in range(nx):
        relay_one(1, q)
        if q == 1:
            for i in range(nx):
                for j in (1, 3, 2):
                    go(mz_copy(j, i))
    flatten_x(1)
    relay_one(2, 0)
    relay_one(2, 1)
    for j in (1, 3, 2):
        for q in range(nx):
            mz_copy(j, q).wait_recv()
    flatten([mz_blk.at[j] for j in range(YS)], mz_flat, 0, HEIGHT, whole)
    stage_a(0)
    stage_a(1)
    relay_one(2, 2)
    stage_b(0)
    relay_one(2, 3)
    stage_b(1)
    relay_one(2, 4)
    flatten_x(2)
    stage_a(2)
    relay_one(3, 0)
    stage_c(0)
    relay_one(3, 1)
    stage_b(2)
    stage_c(1)
    relay_one(3, 2)
    stage_d(0)
    relay_one(3, 3)
    stage_c(2)
    relay_one(3, 4)
    flatten_x(3)
    stage_a(3)
    stage_a(4)
    stage_d(1)
    stage_b(3)
    stage_b(4)
    stage_d(2)
    for q in range(nx):
        relay_one(4, q)
    flatten_x(4)
    stage_a(5)
    stage_c(3)
    stage_b(5)
    stage_c(4)
    stage_e(0)
    stage_d(3)
    stage_c(5)
    stage_e(1)
    stage_d(4)
    stage_e(2)
    stage_e(3)
    early = 4 * TILE
    acc[...] = jnp.dot(gt[:, :early], x_flat[:early, :], preferred_element_type=F32)
    stage_d(5)
    stage_e(4)
    stage_e(5)

    def y_copy(j, q):
        where = (j, slice(None), span_f[q])
        return copy(s1.at[where], r1.at[where], r1_s.at[j, q], r1_r.at[j, q], at_y(j))

    def last_copy(j, q):
        where = (j, slice(None), span_f[q])
        return copy(s2.at[where], r2.at[where], r2_s.at[j, q], r2_r.at[j, q], owner(j))

    def start_ring(q):
        cols = span_f[q]
        total = own[:, cols]
        for j in (1, 3, 2):
            y_copy(j, q).wait_recv()
            total = total + r1[j, :, cols].astype(F32)
        first[:, cols] = total
        f_blk[7, :, cols] = total.astype(BF16)
        go(f_copy(7, q))
        go(f_copy(1, q))

    def first_copy(q):
        where = (slice(None), span_f[q])
        return copy(first.at[where], first_in.at[where], out_s.at[q], out_r.at[q], partner)

    def hand_over(q):
        @pl.when(moves)
        def _():
            first_copy(q).start()

    def finish(q):
        cols = span_f[q]
        for j in (1, 3, 2):
            last_copy(j, q).wait_recv()

        @pl.when(moves)
        def _():
            first_copy(q).wait_recv()
            last_copy(0, q).wait_recv()

        @pl.when(stays)
        def _():
            first_in[:, cols] = first[:, cols]
            r2[0, :, cols] = s2[0, :, cols]

        second = r2[0, :, cols].astype(F32)
        for j in (1, 3, 2):
            second = second + r2[j, :, cols].astype(F32)
        result = coef_a * m_ref[:, cols].astype(F32) + coef_b * first_in[:, cols] + coef_c * second
        o_ref[:, cols] = result.astype(BF16)

    count = len(span_f)

    def product(q):
        cols = span_f[q]
        part = acc[:, cols] + jnp.dot(gt[:, early:], x_flat[early:, cols], preferred_element_type=F32)
        for j in (2, 1, 3):
            s1[j, :, cols] = part[j * ROWS:(j + 1) * ROWS].astype(BF16)
            go(y_copy(j, q))
        own[:, cols] = part[:ROWS]

    def second_product(q):
        cols = span_f[q]
        part = jnp.dot(gt[...], f_flat[:, cols], preferred_element_type=F32)
        for j in (2, 1, 3, 0):
            s2[j, :, cols] = part[j * ROWS:(j + 1) * ROWS].astype(BF16)
            if j > 0:
                go(last_copy(j, q))

        @pl.when(moves)
        def _():
            last_copy(0, q).start()

    def arrive(q, s):
        relay(f_copy, RIGHT_F, s, q)
        slots, start, rows = UNITS[s - 1]
        flatten([f_blk.at[(k - 1) % ZS] for k in slots], f_flat, start, rows, span_f[q])

    act = {
        "p": product, "s": start_ring, "h": hand_over, "r": arrive, "g": second_product,
        "f": finish,
    }
    for step in STEPS:
        act[step[0]](*map(int, step[1:]))
        if step[0] == "r":
            for cp in sends[:5]:
                cp.wait_send()
            del sends[:5]

    @pl.when(moves)
    def _():
        for q in range(nx):
            mz_copy(0, q).wait_send()
        for q in range(count):
            first_copy(q).wait_send()
            last_copy(0, q).wait_send()

    for cp in sends:
        cp.wait_send()


def shards(momentum):
    vm, dma = pltpu.VMEM, pltpu.SemaphoreType.DMA
    blk = (ROWS, COLS)
    tile = (TILES, HEIGHT, LANE)
    scratch = [
        vm((YS,) + blk, BF16), vm((ZS - 1,) + blk, BF16), vm((ZS,) + blk, BF16),
        vm((HEIGHT, COLS), BF16), vm((DEPTH, COLS), BF16), vm((DEPTH, COLS), BF16),
        vm(tile, F32), vm(tile, F32), vm(tile, F32),
        vm((TILES, XS, ROWS, LANE), BF16), vm((TILES, XS - 1, ROWS, LANE), BF16),
        vm((XS, ROWS, DEPTH), BF16), vm((HEIGHT, DEPTH), BF16),
        vm((HEIGHT, COLS), F32), vm(blk, F32), vm(blk, F32), vm(blk, F32),
        vm((YS,) + blk, BF16), vm((YS,) + blk, BF16), vm((YS,) + blk, BF16), vm((YS,) + blk, BF16),
    ]
    nx, nf = len(RING_X), len(RING_F)
    for shape in (
        (YS, nx), (ZS, nx), (ZS, nf), (TILES,), (TILES, 3), (TILES, 3), (TILES,), (YS, nf), (YS, nf),
        (nf,),
    ):
        scratch += [dma(shape), dma(shape)]
    return pl.pallas_call(
        kernel,
        out_shape=jax.ShapeDtypeStruct(blk, BF16),
        in_specs=[pl.BlockSpec(memory_space=pltpu.VMEM)],
        out_specs=pl.BlockSpec(memory_space=pltpu.VMEM),
        scratch_shapes=scratch,
        compiler_params=pltpu.CompilerParams(
            collective_id=0, has_side_effects=True, vmem_limit_bytes=56 * 1024 * 1024
        ),
        name="newton_schulz",
    )(momentum)


def solution(mesh):
    in_specs = (P("row", "col"),)
    out_specs = P("row", "col")
    return jax.shard_map(shards, mesh=mesh, in_specs=in_specs, out_specs=out_specs, check_vma=False)
```

```python
import jax
import jax.numpy as jnp
from jax import lax
from jax.experimental import pallas as pl
from jax.experimental.pallas import tpu as pltpu
from jax.sharding import PartitionSpec as P

BREADTH = 9216
MESH = pl.DeviceIdType.MESH
F32 = jnp.float32
BF16 = jnp.bfloat16

coef_a = 3.4445
coef_b = -4.775
coef_c = 2.0315

ROWS, COLS = 168, 1152
ZS, YS, XS = 8, 4, 4
LANE = 128
RING_X = (1, 2, 2, 2, 2)
RING_F = (1, 1, 1, 1, 2, 2, 1)
RIGHT_X = (1, 2)
RIGHT_F = (0, 1, 2, 3)
STEPS = (
    "p0", "p1", "p2", "p3", "p4", "p5", "p6", "s0", "s1", "r01", "s2", "r11", "s3", "r02", "r21",
    "r12", "r31", "s4", "r03", "r22", "r13", "r32", "s5", "r41", "s6", "h0", "h1", "r04", "g0",
    "r23", "r14", "g1", "h2", "h3", "r33", "r51", "r42", "h4", "r61", "r24", "g2", "r34", "g3",
    "h5", "r52", "r43", "h6", "r44", "r62", "g4", "f0", "f1", "r53", "r54", "g5", "f2", "r63",
    "r64", "g6", "f3", "f4", "f5", "f6",
)
UNITS = (((0, 1, 7), 0, 512), ((2, 6), 512, 384), ((3, 5), 896, 384), ((4,), 1280, 256))
DEPTH = 1536
HEIGHT = YS * ROWS
TILE = 2 * LANE
TILES = DEPTH // TILE


def chunks(widths):
    spans, start = [], 0
    for w in widths:
        spans.append(pl.ds(start * LANE, w * LANE))
        start += w
    return spans


def place(x, y, z, c):
    return (lax.rem(y, 2) * 16 + z * 2 + c, x * 2 + y // 2)


def flatten(blocks, dst, start, rows, cols):
    empty = rows - ROWS * len(blocks)
    for l in range(cols.start, cols.start + cols.size, LANE):
        parts = [blk[:, l:l + LANE].astype(F32) for blk in blocks]
        if empty:
            parts.append(jnp.zeros((empty, LANE), F32))
        stacked = parts[0] if len(parts) == 1 else jnp.concatenate(parts, axis=0)
        dst[start:start + rows, l:l + LANE] = stacked.astype(BF16)


def kernel(
    m_ref, o_ref,
    mz_blk, x_blk, f_blk, mz_flat, x_flat, f_flat,
    ex, er, gsum, gs, gr, gg, gt,
    acc, own, first, first_in, s1, r1, s2, r2,
    mz_s, mz_r, xz_s, xz_r, fz_s, fz_r,
    ex_s, ex_r, gr_s, gr_r, gx_s, gx_r, gc_s, gc_r,
    r1_s, r1_r, r2_s, r2_r, out_s, out_r,
):
    row, col = lax.axis_index("row"), lax.axis_index("col")
    x, y_hi = col // 2, lax.rem(col, 2)
    y_lo, z, c = row // 16, lax.rem(row // 2, ZS), lax.rem(row, 2)
    y = y_hi * 2 + y_lo

    def at_z(d):
        return place(x, y, lax.rem(z + d + ZS, ZS), c)

    def at_y(d):
        return place(x, lax.rem(y + d + YS, YS), z, c)

    def at_x(d):
        return place(lax.rem(x + d + XS, XS), y, z, c)

    other_core = place(x, y, z, 1 - c)
    home = c * 2 + y_lo

    def taker(j):
        return place(x, lax.rem(home - j + YS, YS), z, y_hi)

    partner = taker(0)

    def owner(j):
        to = lax.rem(y + j, YS)
        return place(x, c * 2 + lax.rem(to, 2), z, to // 2)

    stays = c == y_hi
    moves = jnp.logical_not(stays)

    def copy(src, dst, send, recv, to):
        return pltpu.make_async_remote_copy(
            src_ref=src, dst_ref=dst, send_sem=send, recv_sem=recv,
            device_id=to, device_id_type=MESH,
        )

    def sent(ref, sem):
        copy(ref, ref, sem, sem, other_core).wait_send()

    def come(ref, sem):
        copy(ref, ref, sem, sem, other_core).wait_recv()

    barrier = pltpu.get_barrier_semaphore()

    def greet(peer):
        pl.semaphore_signal(barrier, inc=1, device_id=peer, device_id_type=MESH)

    for peer in (
        [at_z(1), at_z(-1), other_core]
        + [at_y(d) for d in (1, 2, 3)] + [at_x(d) for d in (1, 2, 3)]
        + [taker(j) for j in (1, 2, 3)] + [owner(j) for j in (1, 2, 3)]
    ):
        greet(peer)

    @pl.when(moves)
    def _():
        greet(partner)
        pl.semaphore_wait(barrier, 16)

    @pl.when(stays)
    def _():
        pl.semaphore_wait(barrier, 15)

    span_x, span_f = chunks(RING_X), chunks(RING_F)
    nx, count = len(span_x), len(span_f)

    def mz_copy(j, q):
        where = mz_blk.at[j, :, span_x[q]]
        return copy(m_ref.at[:, span_x[q]], where, mz_s.at[min(j, 1)], mz_r.at[q if j == 0 else nx], taker(j))

    @pl.when(stays)
    def _():
        mz_blk[0] = m_ref[...]

    @pl.when(moves)
    def _():
        for q in range(len(span_x)):
            mz_copy(0, q).start()

    def z_copy(own_blk, blk, spans, right, ss, rs, dst, q):
        if dst > 4 or (dst == 4 and q in right):
            src, to = (dst + 1) % ZS, at_z(1)
        else:
            src, to = dst - 1, at_z(-1)
        src_ref = own_blk.at[:, spans[q]] if src == 0 else blk.at[src - 1, :, spans[q]]
        return copy(src_ref, blk.at[dst - 1, :, spans[q]], ss, rs.at[min(dst, ZS - dst), q], to)

    def x_copy(dst, q):
        return z_copy(mz_blk.at[0], x_blk, span_x, RIGHT_X, xz_s, xz_r, dst, q)

    def f_copy(dst, q):
        return z_copy(f_blk.at[7], f_blk, span_f, RIGHT_F, fz_s, fz_r, dst, q)

    def relay(make, right, s, q):
        if s == 4:
            make(4, q).wait_recv()
            return
        blk, rs, spans = (x_blk, xz_r, span_x) if make is x_copy else (f_blk, fz_r, span_f)
        come(blk.at[pl.ds(0, 2), :, spans[q]], rs.at[s, q])
        for nxt, far in ((ZS - s - 1, q in right), (s + 1, q not in right)):
            if s < 3 or far:
                make(nxt, q).start()

    for q in range(len(span_x)):

        @pl.when(moves)
        def _():
            mz_copy(0, q).wait_recv()

        x_copy(7, q).start()
        x_copy(1, q).start()

    whole = pl.ds(0, COLS)

    def lanes(u, core):
        return pl.ds(pl.multiple_of((2 * u + core) * LANE, LANE), LANE)

    def ex_copy(u):
        return copy(ex.at[u], er.at[u], ex_s, ex_r.at[u], other_core)

    def gr_copy(u, d):
        p = lax.rem(x + d, XS)
        return copy(
            gs.at[u, p], gr.at[u, d - 1], gr_s, gr_r.at[u], at_x(d)
        )

    def gx_copy(u, d, p):
        where = gg.at[p, :, lanes(u, c)]
        return copy(where, where, gx_s, gx_r.at[u], at_x(d))

    def gc_copy(u, core):
        where = gg.at[:, :, lanes(u, core)]
        return copy(where, where, gc_s, gc_r.at[u], other_core)

    def flatten_x(s):
        slots, start, rows = UNITS[s - 1]
        blocks = [mz_blk.at[0] if k == 0 else x_blk.at[k - 1] for k in slots]
        flatten(blocks, x_flat, start, rows, whole)

    def relay_one(s, q):
        relay(x_copy, RIGHT_X, s, q)

    def stage_a(u):
        part = lax.dot_general(
            mz_flat[...], x_flat[u * TILE:(u + 1) * TILE, :], (((1,), (1,)), ((), ())),
            preferred_element_type=F32,
        )
        part = part * (1.0 / BREADTH)
        ex[u] = jnp.where(c == 0, part[:, LANE:], part[:, :LANE])
        ex_copy(u).start()
        gsum[u] = jnp.where(c == 0, part[:, :LANE], part[:, LANE:])

    def stage_b(u):
        ex_copy(u).wait_recv()
        total = gsum[u] + er[u]
        gsum[u] = total
        for p in range(XS):
            gs[u, p] = total[p * ROWS:(p + 1) * ROWS].astype(BF16)
        for d in (1, 3, 2):
            gr_copy(u, d).start()

    def stage_c(u):
        come(gr.at[u], gr_r.at[u])
        total = gsum[u, pl.ds(pl.multiple_of(x * ROWS, 8), ROWS), :]
        for d in range(3):
            total = total + gr[u, d].astype(F32)
        gg[x, :, lanes(u, c)] = total.astype(BF16)
        for d in (1, 3, 2):
            gx_copy(u, d, x).start()

    def stage_d(u):
        come(gr.at[u], gx_r.at[u])
        gc_copy(u, c).start()

    def stage_e(u):
        gc_copy(u, 1 - c).wait_recv()
        flatten([gg.at[p] for p in range(XS)], gt, 0, HEIGHT, pl.ds(u * TILE, TILE))

    for q in range(nx):
        relay_one(1, q)
        if q == 1:
            for i in range(nx):
                for j in (1, 3, 2):
                    mz_copy(j, i).start()
    flatten_x(1)
    relay_one(2, 0)
    relay_one(2, 1)
    come(mz_blk.at[pl.ds(1, 3)], mz_r.at[nx])
    flatten([mz_blk.at[j] for j in range(YS)], mz_flat, 0, HEIGHT, whole)
    stage_a(0)
    stage_a(1)
    relay_one(2, 2)
    stage_b(0)
    relay_one(2, 3)
    stage_b(1)
    relay_one(2, 4)
    flatten_x(2)
    stage_a(2)
    relay_one(3, 0)
    stage_c(0)
    relay_one(3, 1)
    stage_b(2)
    stage_c(1)
    relay_one(3, 2)
    stage_d(0)
    relay_one(3, 3)
    stage_c(2)
    relay_one(3, 4)
    flatten_x(3)
    stage_a(3)
    stage_a(4)
    stage_d(1)
    stage_b(3)
    stage_b(4)
    stage_d(2)
    for q in range(nx):
        relay_one(4, q)
    flatten_x(4)
    stage_a(5)
    stage_c(3)
    stage_b(5)
    stage_c(4)
    stage_e(0)
    stage_d(3)
    stage_c(5)
    stage_e(1)
    stage_d(4)
    stage_e(2)
    stage_e(3)
    early = 4 * TILE
    acc[...] = jnp.dot(gt[:, :early], x_flat[:early, :], preferred_element_type=F32)
    stage_d(5)
    stage_e(4)
    stage_e(5)

    def y_copy(j, q):
        where = (j, slice(None), span_f[q])
        return copy(s1.at[where], r1.at[where], r1_s, r1_r.at[q], at_y(j))

    def last_copy(j, q):
        where = (j, slice(None), span_f[q])
        return copy(s2.at[where], r2.at[where], r2_s.at[min(j, 1)], r2_r.at[q], owner(j))

    def start_ring(q):
        cols = span_f[q]
        total = own[:, cols]
        come(r1.at[pl.ds(1, 3), :, cols], r1_r.at[q])
        for j in (1, 3, 2):
            total = total + r1[j, :, cols].astype(F32)
        first[:, cols] = total
        f_blk[7, :, cols] = total.astype(BF16)
        f_copy(7, q).start()
        f_copy(1, q).start()

    def first_copy(q):
        where = (slice(None), span_f[q])
        return copy(first.at[where], first_in.at[where], out_s, out_r.at[q], partner)

    def hand_over(q):
        @pl.when(moves)
        def _():
            first_copy(q).start()

    def finish(q):
        cols = span_f[q]

        @pl.when(moves)
        def _():
            first_copy(q).wait_recv()
            come(r2.at[:, :, cols], r2_r.at[q])

        @pl.when(stays)
        def _():
            come(r2.at[pl.ds(1, 3), :, cols], r2_r.at[q])
            first_in[:, cols] = first[:, cols]
            r2[0, :, cols] = s2[0, :, cols]

        second = r2[0, :, cols].astype(F32)
        for j in (1, 3, 2):
            second = second + r2[j, :, cols].astype(F32)
        result = coef_a * m_ref[:, cols].astype(F32) + coef_b * first_in[:, cols] + coef_c * second
        o_ref[:, cols] = result.astype(BF16)

    def product(q):
        cols = span_f[q]
        part = acc[:, cols] + jnp.dot(gt[:, early:], x_flat[early:, cols], preferred_element_type=F32)
        for j in (2, 1, 3):
            s1[j, :, cols] = part[j * ROWS:(j + 1) * ROWS].astype(BF16)
            y_copy(j, q).start()
        own[:, cols] = part[:ROWS]

    def second_product(q):
        cols = span_f[q]
        part = jnp.dot(gt[...], f_flat[:, cols], preferred_element_type=F32)
        for j in (2, 1, 3, 0):
            s2[j, :, cols] = part[j * ROWS:(j + 1) * ROWS].astype(BF16)
            if j > 0:
                last_copy(j, q).start()

        @pl.when(moves)
        def _():
            last_copy(0, q).start()

    def arrive(q, s):
        relay(f_copy, RIGHT_F, s, q)
        slots, start, rows = UNITS[s - 1]
        flatten([f_blk.at[(k - 1) % ZS] for k in slots], f_flat, start, rows, span_f[q])

    act = {
        "p": product, "s": start_ring, "h": hand_over, "r": arrive, "g": second_product,
        "f": finish,
    }
    for step in STEPS:
        act[step[0]](*map(int, step[1:]))

    @pl.when(moves)
    def _():
        sent(mz_blk.at[0], mz_s.at[0])
        sent(first, out_s)
        sent(s2.at[0], r2_s.at[0])

    three = pl.ds(0, 3)
    sent(mz_blk.at[three], mz_s.at[1])
    sent(x_blk, xz_s)
    sent(ex, ex_s)
    sent(gs.at[:, three], gr_s)
    sent(gs.at[:, three], gx_s)
    sent(gs, gc_s)
    sent(s1.at[three], r1_s)
    sent(f_blk.at[pl.ds(0, ZS - 1)], fz_s)
    sent(s2.at[three], r2_s.at[1])


def shards(momentum):
    vm, dma = pltpu.VMEM, pltpu.SemaphoreType.DMA
    blk = (ROWS, COLS)
    tile = (TILES, HEIGHT, LANE)
    scratch = [
        vm((YS,) + blk, BF16), vm((ZS - 1,) + blk, BF16), vm((ZS,) + blk, BF16),
        vm((HEIGHT, COLS), BF16), vm((DEPTH, COLS), BF16), vm((DEPTH, COLS), BF16),
        vm(tile, F32), vm(tile, F32), vm(tile, F32),
        vm((TILES, XS, ROWS, LANE), BF16), vm((TILES, XS - 1, ROWS, LANE), BF16),
        vm((XS, ROWS, DEPTH), BF16), vm((HEIGHT, DEPTH), BF16),
        vm((HEIGHT, COLS), F32), vm(blk, F32), vm(blk, F32), vm(blk, F32),
        vm((YS,) + blk, BF16), vm((YS,) + blk, BF16), vm((YS,) + blk, BF16), vm((YS,) + blk, BF16),
    ]
    nx, nf = len(RING_X), len(RING_F)
    for shape in (
        (2,), (nx + 1,), (), (5, nx), (), (5, nf), (), (TILES,), (), (TILES,), (), (TILES,),
        (), (TILES,), (), (nf,), (2,), (nf,), (), (nf,),
    ):
        scratch.append(dma(shape))
    return pl.pallas_call(
        kernel,
        out_shape=jax.ShapeDtypeStruct(blk, BF16),
        in_specs=[pl.BlockSpec(memory_space=pltpu.VMEM)],
        out_specs=pl.BlockSpec(memory_space=pltpu.VMEM),
        scratch_shapes=scratch,
        compiler_params=pltpu.CompilerParams(
            collective_id=0, has_side_effects=True, vmem_limit_bytes=56 * 1024 * 1024
        ),
        name="newton_schulz",
    )(momentum)


def solution(mesh):
    in_specs = (P("row", "col"),)
    out_specs = P("row", "col")
    return jax.shard_map(shards, mesh=mesh, in_specs=in_specs, out_specs=out_specs, check_vma=False)
```

```python
import jax
import jax.numpy as jnp
from jax import lax
from jax.experimental import pallas as pl
from jax.experimental.pallas import tpu as pltpu
from jax.sharding import PartitionSpec as P

BREADTH = 9216
MESH = pl.DeviceIdType.MESH
F32 = jnp.float32
BF16 = jnp.bfloat16

coef_a = 3.4445
coef_b = -4.775
coef_c = 2.0315

ROWS, COLS = 168, 1152
ZS, YS, XS = 8, 4, 4
LANE = 128
RING_X = (1, 1, 2, 2, 3)
RING_F = (1, 1, 1, 1, 2, 2, 1)
RIGHT_X = (2, 3)
RIGHT_F = (0, 1, 2, 3)
STEPS = (
    "p0", "p1", "p2", "p3", "p4", "p5", "p6", "s0", "s1", "r01", "s2", "r11", "s3", "r02", "r21",
    "r12", "r31", "s4", "r03", "r22", "r13", "r32", "s5", "r41", "s6", "h0", "h1", "r04", "g0",
    "r23", "r14", "g1", "h2", "h3", "r33", "r51", "r42", "h4", "r61", "r24", "g2", "r34", "g3",
    "h5", "r52", "r43", "h6", "r44", "r62", "g4", "f0", "f1", "r53", "r54", "g5", "f2", "r63",
    "r64", "g6", "f3", "f4", "f5", "f6",
)
NEAR, FAR = (0, 1, 3), (2,)
UNITS = (((0, 1, 7), 0, 512), ((2, 6), 512, 384), ((3, 5), 896, 384), ((4,), 1280, 256))
DEPTH = 1536
HEIGHT = YS * ROWS
TILE = 2 * LANE
TILES = DEPTH // TILE


def chunks(widths):
    spans, start = [], 0
    for w in widths:
        spans.append(pl.ds(start * LANE, w * LANE))
        start += w
    return spans


def place(x, y, z, c):
    return (lax.rem(y, 2) * 16 + z * 2 + c, x * 2 + y // 2)


def flatten(blocks, dst, start, rows, cols):
    empty = rows - ROWS * len(blocks)
    for l in range(cols.start, cols.start + cols.size, LANE):
        parts = [blk[:, l:l + LANE].astype(F32) for blk in blocks]
        if empty:
            parts.append(jnp.zeros((empty, LANE), F32))
        stacked = parts[0] if len(parts) == 1 else jnp.concatenate(parts, axis=0)
        dst[start:start + rows, l:l + LANE] = stacked.astype(BF16)


def kernel(
    m_ref, o_ref,
    mz_blk, x_blk, f_blk, mz_flat, x_flat, f_flat,
    ex, er, gsum, gs, gr, gg, gt,
    acc, own, first, first_in, s1, r1, s2, r2,
    mz_s, mz_r, xz_s, xz_r, fz_s, fz_r,
    ex_s, ex_r, gr_s, gr_r, gx_s, gx_r, gc_s, gc_r,
    r1_s, r1_r, r2_s, r2_r, out_s, out_r,
):
    row, col = lax.axis_index("row"), lax.axis_index("col")
    x, y_hi = col // 2, lax.rem(col, 2)
    y_lo, z, c = row // 16, lax.rem(row // 2, ZS), lax.rem(row, 2)
    y = y_hi * 2 + y_lo

    def at_z(d):
        return place(x, y, lax.rem(z + d + ZS, ZS), c)

    def at_y(d):
        return place(x, lax.rem(y + d + YS, YS), z, c)

    def at_x(d):
        return place(lax.rem(x + d + XS, XS), y, z, c)

    other_core = place(x, y, z, 1 - c)
    home = c * 2 + y_lo

    def taker(j):
        return place(x, lax.rem(home - j + YS, YS), z, y_hi)

    partner = taker(0)

    def owner(j):
        to = lax.rem(y + j, YS)
        return place(x, c * 2 + lax.rem(to, 2), z, to // 2)

    stays = c == y_hi
    moves = jnp.logical_not(stays)

    def copy(src, dst, send, recv, to):
        return pltpu.make_async_remote_copy(
            src_ref=src, dst_ref=dst, send_sem=send, recv_sem=recv,
            device_id=to, device_id_type=MESH,
        )

    def sent(ref, sem):
        copy(ref, ref, sem, sem, other_core).wait_send()

    def come(ref, sem):
        copy(ref, ref, sem, sem, other_core).wait_recv()

    barrier = pltpu.get_barrier_semaphore()

    def greet(peer):
        pl.semaphore_signal(barrier, inc=1, device_id=peer, device_id_type=MESH)

    for peer in (
        [at_z(1), at_z(-1), other_core]
        + [at_y(d) for d in (1, 2, 3)] + [at_x(d) for d in (1, 2, 3)]
        + [taker(j) for j in (1, 2, 3)] + [owner(j) for j in (1, 2, 3)]
    ):
        greet(peer)

    @pl.when(moves)
    def _():
        greet(partner)
        pl.semaphore_wait(barrier, 16)

    @pl.when(stays)
    def _():
        pl.semaphore_wait(barrier, 15)

    span_x, span_f = chunks(RING_X), chunks(RING_F)
    nx, count = len(span_x), len(span_f)

    def mz_copy(j, q):
        where = mz_blk.at[j, :, span_x[q]]
        return copy(m_ref.at[:, span_x[q]], where, mz_s.at[min(j, 1)], mz_r.at[q if j == 0 else nx + (j == 2)], taker(j))

    @pl.when(stays)
    def _():
        mz_blk[0] = m_ref[...]

    @pl.when(moves)
    def _():
        for q in range(len(span_x)):
            mz_copy(0, q).start()

    def z_copy(own_blk, blk, spans, right, ss, rs, dst, q):
        if dst > 4 or (dst == 4 and q in right):
            src, to = (dst + 1) % ZS, at_z(1)
        else:
            src, to = dst - 1, at_z(-1)
        src_ref = own_blk.at[:, spans[q]] if src == 0 else blk.at[src - 1, :, spans[q]]
        return copy(src_ref, blk.at[dst - 1, :, spans[q]], ss, rs.at[min(dst, ZS - dst), q], to)

    def x_copy(dst, q):
        return z_copy(mz_blk.at[0], x_blk, span_x, RIGHT_X, xz_s, xz_r, dst, q)

    def f_copy(dst, q):
        return z_copy(f_blk.at[7], f_blk, span_f, RIGHT_F, fz_s, fz_r, dst, q)

    def relay(make, right, s, q):
        if s == 4:
            make(4, q).wait_recv()
            return
        blk, rs, spans = (x_blk, xz_r, span_x) if make is x_copy else (f_blk, fz_r, span_f)
        come(blk.at[pl.ds(0, 2), :, spans[q]], rs.at[s, q])
        for nxt, far in ((ZS - s - 1, q in right), (s + 1, q not in right)):
            if s < 3 or far:
                make(nxt, q).start()

    for q in range(len(span_x)):

        @pl.when(moves)
        def _():
            mz_copy(0, q).wait_recv()

        x_copy(7, q).start()
        x_copy(1, q).start()

    whole = pl.ds(0, COLS)

    def lanes(u, core):
        return pl.ds(pl.multiple_of((2 * u + core) * LANE, LANE), LANE)

    def ex_copy(u):
        return copy(ex.at[u], er.at[u], ex_s, ex_r.at[u], other_core)

    def gr_copy(u, d):
        p = lax.rem(x + d, XS)
        return copy(
            gs.at[u, p], gr.at[u, d - 1], gr_s, gr_r.at[u], at_x(d)
        )

    def gx_copy(u, d, p):
        where = gg.at[p, :, lanes(u, c)]
        return copy(where, where, gx_s, gx_r.at[u], at_x(d))

    def gc_copy(u, core):
        where = gg.at[:, :, lanes(u, core)]
        return copy(where, where, gc_s, gc_r.at[u], other_core)

    def flatten_x(s):
        slots, start, rows = UNITS[s - 1]
        blocks = [mz_blk.at[0] if k == 0 else x_blk.at[k - 1] for k in slots]
        flatten(blocks, x_flat, start, rows, whole)

    def relay_one(s, q):
        relay(x_copy, RIGHT_X, s, q)

    def stage_a(u):
        part = lax.dot_general(
            mz_flat[...], x_flat[u * TILE:(u + 1) * TILE, :], (((1,), (1,)), ((), ())),
            preferred_element_type=F32,
        )
        part = part * (1.0 / BREADTH)
        ex[u] = jnp.where(c == 0, part[:, LANE:], part[:, :LANE])
        ex_copy(u).start()
        gsum[u] = jnp.where(c == 0, part[:, :LANE], part[:, LANE:])

    def block_rows(j):
        return slice(j * ROWS, (j + 1) * ROWS)

    def part_copy(u, rows, far):
        return copy(ex.at[u, rows], er.at[u, rows], ex_s, ex_r.at[far * TILES + u], other_core)

    def parts_a(u, js, sends):
        for j in js:
            part = lax.dot_general(
                mz_blk[j], x_flat[u * TILE:(u + 1) * TILE, :], (((1,), (1,)), ((), ())),
                preferred_element_type=F32,
            )
            part = part * (1.0 / BREADTH)
            ex[u, block_rows(j), :] = jnp.where(c == 0, part[:, LANE:], part[:, :LANE])
            gsum[u, block_rows(j), :] = jnp.where(c == 0, part[:, :LANE], part[:, LANE:])
        for rows in sends:
            part_copy(u, rows, js == FAR).start()

    def parts_b(u, js):
        some = pl.ds(0, ROWS * len(js))
        come(er.at[u, some], ex_r.at[(js == FAR) * TILES + u])
        for j in js:
            total = gsum[u, block_rows(j), :] + er[u, block_rows(j), :]
            gsum[u, block_rows(j), :] = total
            gs[u, j] = total.astype(BF16)

            @pl.when(x != j)
            def _():
                slot = lax.rem(j - x + XS, XS) - 1
                copy(gs.at[u, j], gr.at[u, slot], gr_s, gr_r.at[u], place(j, y, z, c)).start()

    def parts_c(u, js):
        ours = x == 2 if js == FAR else x != 2

        @pl.when(ours)
        def _():
            stage_c(u)

    def near_a(u):
        parts_a(u, NEAR, (pl.ds(0, 2 * ROWS), pl.ds(3 * ROWS, ROWS)))

    def far_a(u):
        parts_a(u, FAR, (pl.ds(2 * ROWS, ROWS),))

    def stage_b(u):
        ex_copy(u).wait_recv()
        total = gsum[u] + er[u]
        gsum[u] = total
        for p in range(XS):
            gs[u, p] = total[p * ROWS:(p + 1) * ROWS].astype(BF16)
        for d in (1, 3, 2):
            gr_copy(u, d).start()

    def stage_c(u):
        come(gr.at[u], gr_r.at[u])
        total = gsum[u, pl.ds(pl.multiple_of(x * ROWS, 8), ROWS), :]
        for d in range(3):
            total = total + gr[u, d].astype(F32)
        gg[x, :, lanes(u, c)] = total.astype(BF16)
        for d in (1, 3, 2):
            gx_copy(u, d, x).start()

    def stage_d(u):
        come(gr.at[u], gx_r.at[u])
        gc_copy(u, c).start()

    def stage_e(u):
        gc_copy(u, 1 - c).wait_recv()
        flatten([gg.at[p] for p in range(XS)], gt, 0, HEIGHT, pl.ds(u * TILE, TILE))

    for q in range(nx):
        relay_one(1, q)
        if q == 1:
            for i in range(nx):
                for j in (1, 3):
                    mz_copy(j, i).start()
    flatten_x(1)
    come(mz_blk.at[pl.ds(1, 2)], mz_r.at[nx])
    for i in range(nx):
        mz_copy(2, i).start()
    near_a(0)
    relay_one(2, 0)
    near_a(1)
    relay_one(2, 1)
    parts_b(0, NEAR)
    parts_b(1, NEAR)
    relay_one(2, 2)
    relay_one(2, 3)
    come(mz_blk.at[2], mz_r.at[nx + 1])
    far_a(0)
    far_a(1)
    flatten([mz_blk.at[j] for j in range(YS)], mz_flat, 0, HEIGHT, whole)
    parts_c(0, NEAR)
    relay_one(2, 4)
    flatten_x(2)
    stage_a(2)
    parts_b(0, FAR)
    parts_b(1, FAR)
    parts_c(1, NEAR)
    relay_one(3, 0)
    relay_one(3, 1)
    stage_b(2)
    relay_one(3, 2)
    relay_one(3, 3)
    relay_one(3, 4)
    flatten_x(3)
    stage_a(3)
    stage_a(4)
    parts_c(0, FAR)
    parts_c(1, FAR)
    stage_b(3)
    stage_b(4)
    stage_c(2)
    stage_d(0)
    stage_d(1)
    for q in range(nx):
        relay_one(4, q)
    flatten_x(4)
    stage_a(5)
    stage_c(3)
    stage_b(5)
    stage_d(2)
    stage_c(4)
    stage_e(0)
    stage_e(1)
    stage_d(3)
    stage_c(5)
    stage_e(2)
    stage_d(4)
    stage_e(3)
    early = 4 * TILE
    acc[...] = jnp.dot(gt[:, :early], x_flat[:early, :], preferred_element_type=F32)
    stage_d(5)
    stage_e(4)
    stage_e(5)

    def y_copy(j, q):
        where = (j, slice(None), span_f[q])
        return copy(s1.at[where], r1.at[where], r1_s, r1_r.at[q], at_y(j))

    def last_copy(j, q):
        where = (j, slice(None), span_f[q])
        return copy(s2.at[where], r2.at[where], r2_s.at[min(j, 1)], r2_r.at[q], owner(j))

    def start_ring(q):
        cols = span_f[q]
        total = own[:, cols]
        come(r1.at[pl.ds(1, 3), :, cols], r1_r.at[q])
        for j in (1, 3, 2):
            total = total + r1[j, :, cols].astype(F32)
        first[:, cols] = total
        f_blk[7, :, cols] = total.astype(BF16)
        f_copy(7, q).start()
        f_copy(1, q).start()

    def first_copy(q):
        where = (slice(None), span_f[q])
        return copy(first.at[where], first_in.at[where], out_s, out_r.at[q], partner)

    def hand_over(q):
        @pl.when(moves)
        def _():
            first_copy(q).start()

    def finish(q):
        cols = span_f[q]

        @pl.when(moves)
        def _():
            first_copy(q).wait_recv()
            come(r2.at[:, :, cols], r2_r.at[q])

        @pl.when(stays)
        def _():
            come(r2.at[pl.ds(1, 3), :, cols], r2_r.at[q])
            first_in[:, cols] = first[:, cols]
            r2[0, :, cols] = s2[0, :, cols]

        second = r2[0, :, cols].astype(F32)
        for j in (1, 3, 2):
            second = second + r2[j, :, cols].astype(F32)
        result = coef_a * m_ref[:, cols].astype(F32) + coef_b * first_in[:, cols] + coef_c * second
        o_ref[:, cols] = result.astype(BF16)

    def product(q):
        cols = span_f[q]
        part = acc[:, cols] + jnp.dot(gt[:, early:], x_flat[early:, cols], preferred_element_type=F32)
        for j in (2, 1, 3):
            s1[j, :, cols] = part[j * ROWS:(j + 1) * ROWS].astype(BF16)
            y_copy(j, q).start()
        own[:, cols] = part[:ROWS]

    def second_product(q):
        cols = span_f[q]
        part = jnp.dot(gt[...], f_flat[:, cols], preferred_element_type=F32)
        for j in (2, 1, 3, 0):
            s2[j, :, cols] = part[j * ROWS:(j + 1) * ROWS].astype(BF16)
            if j > 0:
                last_copy(j, q).start()

        @pl.when(moves)
        def _():
            last_copy(0, q).start()

    def arrive(q, s):
        relay(f_copy, RIGHT_F, s, q)
        slots, start, rows = UNITS[s - 1]
        flatten([f_blk.at[(k - 1) % ZS] for k in slots], f_flat, start, rows, span_f[q])

    act = {
        "p": product, "s": start_ring, "h": hand_over, "r": arrive, "g": second_product,
        "f": finish,
    }
    for step in STEPS:
        act[step[0]](*map(int, step[1:]))

    @pl.when(moves)
    def _():
        sent(mz_blk.at[0], mz_s.at[0])
        sent(first, out_s)
        sent(s2.at[0], r2_s.at[0])

    three = pl.ds(0, 3)
    sent(mz_blk.at[three], mz_s.at[1])
    sent(x_blk, xz_s)
    sent(ex, ex_s)
    sent(gs.at[:, three], gr_s)
    sent(gs.at[:, three], gx_s)
    sent(gs, gc_s)
    sent(s1.at[three], r1_s)
    sent(f_blk.at[pl.ds(0, ZS - 1)], fz_s)
    sent(s2.at[three], r2_s.at[1])


def shards(momentum):
    vm, dma = pltpu.VMEM, pltpu.SemaphoreType.DMA
    blk = (ROWS, COLS)
    tile = (TILES, HEIGHT, LANE)
    scratch = [
        vm((YS,) + blk, BF16), vm((ZS - 1,) + blk, BF16), vm((ZS,) + blk, BF16),
        vm((HEIGHT, COLS), BF16), vm((DEPTH, COLS), BF16), vm((DEPTH, COLS), BF16),
        vm(tile, F32), vm(tile, F32), vm(tile, F32),
        vm((TILES, XS, ROWS, LANE), BF16), vm((TILES, XS - 1, ROWS, LANE), BF16),
        vm((XS, ROWS, DEPTH), BF16), vm((HEIGHT, DEPTH), BF16),
        vm((HEIGHT, COLS), F32), vm(blk, F32), vm(blk, F32), vm(blk, F32),
        vm((YS,) + blk, BF16), vm((YS,) + blk, BF16), vm((YS,) + blk, BF16), vm((YS,) + blk, BF16),
    ]
    nx, nf = len(RING_X), len(RING_F)
    for shape in (
        (2,), (nx + 2,), (), (5, nx), (), (5, nf), (), (2 * TILES,), (), (TILES,), (), (TILES,),
        (), (TILES,), (), (nf,), (2,), (nf,), (), (nf,),
    ):
        scratch.append(dma(shape))
    return pl.pallas_call(
        kernel,
        out_shape=jax.ShapeDtypeStruct(blk, BF16),
        in_specs=[pl.BlockSpec(memory_space=pltpu.VMEM)],
        out_specs=pl.BlockSpec(memory_space=pltpu.VMEM),
        scratch_shapes=scratch,
        compiler_params=pltpu.CompilerParams(
            collective_id=0, has_side_effects=True, vmem_limit_bytes=56 * 1024 * 1024
        ),
        name="newton_schulz",
    )(momentum)


def solution(mesh):
    in_specs = (P("row", "col"),)
    out_specs = P("row", "col")
    return jax.shard_map(shards, mesh=mesh, in_specs=in_specs, out_specs=out_specs, check_vma=False)
```

```python
import jax
import jax.numpy as jnp
from jax import lax
from jax.experimental import pallas as pl
from jax.experimental.pallas import tpu as pltpu
from jax.sharding import PartitionSpec as P

BREADTH = 9216
MESH = pl.DeviceIdType.MESH
F32 = jnp.float32
BF16 = jnp.bfloat16

coef_a = 3.4445
coef_b = -4.775
coef_c = 2.0315

ROWS, COLS = 168, 1152
ZS, YS, XS = 8, 4, 4
LANE = 128
RING_X = (1, 1, 2, 2, 3)
RING_F = (1, 1, 1, 1, 2, 2, 1)
RIGHT_X = (2, 3)
RIGHT_F = (0, 1, 2, 5)
STEPS = (
    "p0", "p1", "p2", "p3", "p4", "p5", "p6", "s0", "s1", "r01", "s2", "r11", "s3", "r02", "r21",
    "r12", "r31", "s4", "r03", "r22", "r13", "r32", "s5", "r41", "s6", "h0", "h1", "r23", "r04", "g0",
    "h2", "h3", "r33", "r14", "g1", "r51", "r42", "h4", "r61", "r24", "g2", "h5", "r52", "r34", "g3",
    "r43", "h6", "r62", "r53", "r44", "g4", "r63", "r54", "g5", "f0", "f1", "f2", "r64", "g6", "f3",
    "f4", "f5", "f6",
)
NEAR, FAR = (0, 1, 3), (2,)
UNITS = (((0, 1, 7), 0, 512), ((2, 6), 512, 384), ((3, 5), 896, 384), ((4,), 1280, 256))
DEPTH = 1536
HEIGHT = YS * ROWS
TILE = 2 * LANE
TILES = DEPTH // TILE


def chunks(widths):
    spans, start = [], 0
    for w in widths:
        spans.append(pl.ds(start * LANE, w * LANE))
        start += w
    return spans


def place(x, y, z, c):
    return (lax.rem(y, 2) * 16 + z * 2 + c, x * 2 + y // 2)


def flatten(blocks, dst, start, rows, cols):
    empty = rows - ROWS * len(blocks)
    for l in range(cols.start, cols.start + cols.size, LANE):
        parts = [blk[:, l:l + LANE].astype(F32) for blk in blocks]
        if empty:
            parts.append(jnp.zeros((empty, LANE), F32))
        stacked = parts[0] if len(parts) == 1 else jnp.concatenate(parts, axis=0)
        dst[start:start + rows, l:l + LANE] = stacked.astype(BF16)


def kernel(
    m_ref, o_ref,
    mz_blk, x_blk, f_blk, mz_flat, x_flat, f_flat,
    ex, er, gsum, gs, gr, gg, gt,
    acc, own, first, first_in, s1, r1, s2, r2,
    mz_s, mz_r, xz_s, xz_r, fz_s, fz_r,
    ex_s, ex_r, gr_s, gr_r, gx_s, gx_r, gc_s, gc_r,
    r1_s, r1_r, r2_s, r2_r, out_s, out_r,
):
    row, col = lax.axis_index("row"), lax.axis_index("col")
    x, y_hi = col // 2, lax.rem(col, 2)
    y_lo, z, c = row // 16, lax.rem(row // 2, ZS), lax.rem(row, 2)
    y = y_hi * 2 + y_lo

    def at_z(d):
        return place(x, y, lax.rem(z + d + ZS, ZS), c)

    def at_y(d):
        return place(x, lax.rem(y + d + YS, YS), z, c)

    def at_x(d):
        return place(lax.rem(x + d + XS, XS), y, z, c)

    other_core = place(x, y, z, 1 - c)
    home = c * 2 + y_lo

    def taker(j):
        return place(x, lax.rem(home - j + YS, YS), z, y_hi)

    partner = taker(0)

    def owner(j):
        to = lax.rem(y + j, YS)
        return place(x, c * 2 + lax.rem(to, 2), z, to // 2)

    stays = c == y_hi
    moves = jnp.logical_not(stays)

    def copy(src, dst, send, recv, to):
        return pltpu.make_async_remote_copy(
            src_ref=src, dst_ref=dst, send_sem=send, recv_sem=recv,
            device_id=to, device_id_type=MESH,
        )

    def sent(ref, sem):
        copy(ref, ref, sem, sem, other_core).wait_send()

    def come(ref, sem):
        copy(ref, ref, sem, sem, other_core).wait_recv()

    barrier = pltpu.get_barrier_semaphore()

    def greet(peer):
        pl.semaphore_signal(barrier, inc=1, device_id=peer, device_id_type=MESH)

    for peer in (
        [at_z(1), at_z(-1), other_core]
        + [at_y(d) for d in (1, 2, 3)] + [at_x(d) for d in (1, 2, 3)]
        + [taker(j) for j in (1, 2, 3)] + [owner(j) for j in (1, 2, 3)]
    ):
        greet(peer)

    @pl.when(moves)
    def _():
        greet(partner)
        pl.semaphore_wait(barrier, 16)

    @pl.when(stays)
    def _():
        pl.semaphore_wait(barrier, 15)

    span_x, span_f = chunks(RING_X), chunks(RING_F)
    nx, count = len(span_x), len(span_f)

    def mz_copy(j, q):
        where = mz_blk.at[j, :, span_x[q]]
        return copy(m_ref.at[:, span_x[q]], where, mz_s.at[min(j, 1)], mz_r.at[q if j == 0 else nx + (j == 2)], taker(j))

    @pl.when(stays)
    def _():
        mz_blk[0] = m_ref[...]

    @pl.when(moves)
    def _():
        for q in range(len(span_x)):
            mz_copy(0, q).start()

    def z_copy(own_blk, blk, spans, right, ss, rs, dst, q):
        if dst > 4 or (dst == 4 and q in right):
            src, to = (dst + 1) % ZS, at_z(1)
        else:
            src, to = dst - 1, at_z(-1)
        src_ref = own_blk.at[:, spans[q]] if src == 0 else blk.at[src - 1, :, spans[q]]
        return copy(src_ref, blk.at[dst - 1, :, spans[q]], ss, rs.at[min(dst, ZS - dst), q], to)

    def x_copy(dst, q):
        return z_copy(mz_blk.at[0], x_blk, span_x, RIGHT_X, xz_s, xz_r, dst, q)

    def f_copy(dst, q):
        return z_copy(f_blk.at[7], f_blk, span_f, RIGHT_F, fz_s, fz_r, dst, q)

    def relay(make, right, s, q):
        if s == 4:
            make(4, q).wait_recv()
            return
        blk, rs, spans = (x_blk, xz_r, span_x) if make is x_copy else (f_blk, fz_r, span_f)
        come(blk.at[pl.ds(0, 2), :, spans[q]], rs.at[s, q])
        for nxt, far in ((ZS - s - 1, q in right), (s + 1, q not in right)):
            if s < 3 or far:
                make(nxt, q).start()

    for q in range(len(span_x)):

        @pl.when(moves)
        def _():
            mz_copy(0, q).wait_recv()

        x_copy(7, q).start()
        x_copy(1, q).start()

    whole = pl.ds(0, COLS)

    def lanes(u, core):
        return pl.ds(pl.multiple_of((2 * u + core) * LANE, LANE), LANE)

    def ex_copy(u):
        return copy(ex.at[u], er.at[u], ex_s, ex_r.at[u], other_core)

    def gr_copy(u, d):
        p = lax.rem(x + d, XS)
        return copy(
            gs.at[u, p], gr.at[u, d - 1], gr_s, gr_r.at[u], at_x(d)
        )

    def gx_copy(u, d, p):
        where = gg.at[p, :, lanes(u, c)]
        return copy(where, where, gx_s, gx_r.at[u], at_x(d))

    def gc_copy(u, core):
        where = gg.at[:, :, lanes(u, core)]
        return copy(where, where, gc_s, gc_r.at[u], other_core)

    def flatten_x(s):
        slots, start, rows = UNITS[s - 1]
        blocks = [mz_blk.at[0] if k == 0 else x_blk.at[k - 1] for k in slots]
        flatten(blocks, x_flat, start, rows, whole)

    def relay_one(s, q):
        relay(x_copy, RIGHT_X, s, q)

    def stage_a(u):
        part = lax.dot_general(
            mz_flat[...], x_flat[u * TILE:(u + 1) * TILE, :], (((1,), (1,)), ((), ())),
            preferred_element_type=F32,
        )
        part = part * (1.0 / BREADTH)
        ex[u] = jnp.where(c == 0, part[:, LANE:], part[:, :LANE])
        ex_copy(u).start()
        gsum[u] = jnp.where(c == 0, part[:, :LANE], part[:, LANE:])

    def block_rows(j):
        return slice(j * ROWS, (j + 1) * ROWS)

    def part_copy(u, rows, far):
        return copy(ex.at[u, rows], er.at[u, rows], ex_s, ex_r.at[far * TILES + u], other_core)

    def parts_a(u, js, sends):
        for j in js:
            part = lax.dot_general(
                mz_blk[j], x_flat[u * TILE:(u + 1) * TILE, :], (((1,), (1,)), ((), ())),
                preferred_element_type=F32,
            )
            part = part * (1.0 / BREADTH)
            ex[u, block_rows(j), :] = jnp.where(c == 0, part[:, LANE:], part[:, :LANE])
            gsum[u, block_rows(j), :] = jnp.where(c == 0, part[:, :LANE], part[:, LANE:])
        for rows in sends:
            part_copy(u, rows, js == FAR).start()

    def parts_b(u, js):
        some = pl.ds(0, ROWS * len(js))
        come(er.at[u, some], ex_r.at[(js == FAR) * TILES + u])
        for j in js:
            total = gsum[u, block_rows(j), :] + er[u, block_rows(j), :]
            gsum[u, block_rows(j), :] = total
            gs[u, j] = total.astype(BF16)

            @pl.when(x != j)
            def _():
                slot = lax.rem(j - x + XS, XS) - 1
                copy(gs.at[u, j], gr.at[u, slot], gr_s, gr_r.at[u], place(j, y, z, c)).start()

    def parts_c(u, js):
        ours = x == 2 if js == FAR else x != 2

        @pl.when(ours)
        def _():
            stage_c(u)

    def near_a(u):
        parts_a(u, NEAR, (pl.ds(0, 2 * ROWS), pl.ds(3 * ROWS, ROWS)))

    def far_a(u):
        parts_a(u, FAR, (pl.ds(2 * ROWS, ROWS),))

    def stage_b(u):
        ex_copy(u).wait_recv()
        total = gsum[u] + er[u]
        gsum[u] = total
        for p in range(XS):
            gs[u, p] = total[p * ROWS:(p + 1) * ROWS].astype(BF16)
        for d in (1, 3, 2):
            gr_copy(u, d).start()

    def stage_c(u):
        come(gr.at[u], gr_r.at[u])
        total = gsum[u, pl.ds(pl.multiple_of(x * ROWS, 8), ROWS), :]
        for d in range(3):
            total = total + gr[u, d].astype(F32)
        gg[x, :, lanes(u, c)] = total.astype(BF16)
        for d in (1, 3, 2):
            gx_copy(u, d, x).start()

    def stage_d(u):
        come(gr.at[u], gx_r.at[u])
        gc_copy(u, c).start()

    def stage_e(u):
        gc_copy(u, 1 - c).wait_recv()
        flatten([gg.at[p] for p in range(XS)], gt, 0, HEIGHT, pl.ds(u * TILE, TILE))

    for q in range(nx):
        relay_one(1, q)
        if q == 1:
            for i in range(nx):
                for j in (1, 3):
                    mz_copy(j, i).start()
    flatten_x(1)
    come(mz_blk.at[pl.ds(1, 2)], mz_r.at[nx])
    for i in range(nx):
        mz_copy(2, i).start()
    near_a(0)
    relay_one(2, 0)
    near_a(1)
    relay_one(2, 1)
    parts_b(0, NEAR)
    parts_b(1, NEAR)
    relay_one(2, 2)
    relay_one(2, 3)
    come(mz_blk.at[2], mz_r.at[nx + 1])
    far_a(0)
    far_a(1)
    flatten([mz_blk.at[j] for j in range(YS)], mz_flat, 0, HEIGHT, whole)
    parts_c(0, NEAR)
    relay_one(2, 4)
    flatten_x(2)
    stage_a(2)
    parts_b(0, FAR)
    parts_b(1, FAR)
    parts_c(1, NEAR)
    relay_one(3, 0)
    relay_one(3, 1)
    stage_b(2)
    relay_one(3, 2)
    relay_one(3, 3)
    relay_one(3, 4)
    flatten_x(3)
    stage_a(3)
    stage_a(4)
    parts_c(0, FAR)
    parts_c(1, FAR)
    stage_b(3)
    stage_b(4)
    stage_c(2)
    stage_d(0)
    stage_d(1)
    for q in range(nx):
        relay_one(4, q)
    flatten_x(4)
    stage_a(5)
    stage_c(3)
    stage_b(5)
    stage_d(2)
    stage_c(4)
    stage_e(0)
    stage_e(1)
    stage_d(3)
    stage_c(5)
    stage_e(2)
    stage_d(4)
    stage_e(3)
    early = 4 * TILE
    acc[...] = jnp.dot(gt[:, :early], x_flat[:early, :], preferred_element_type=F32)
    stage_d(5)
    stage_e(4)
    stage_e(5)

    def y_copy(j, q):
        where = (j, slice(None), span_f[q])
        return copy(s1.at[where], r1.at[where], r1_s, r1_r.at[q], at_y(j))

    def last_copy(j, q):
        where = (j, slice(None), span_f[q])
        return copy(s2.at[where], r2.at[where], r2_s.at[min(j, 1)], r2_r.at[q], owner(j))

    def start_ring(q):
        cols = span_f[q]
        total = own[:, cols]
        come(r1.at[pl.ds(1, 3), :, cols], r1_r.at[q])
        for j in (1, 3, 2):
            total = total + r1[j, :, cols].astype(F32)
        first[:, cols] = total
        f_blk[7, :, cols] = total.astype(BF16)
        f_copy(7, q).start()
        f_copy(1, q).start()

    def first_copy(q):
        where = (slice(None), span_f[q])
        return copy(first.at[where], first_in.at[where], out_s, out_r.at[q], partner)

    def hand_over(q):
        @pl.when(moves)
        def _():
            first_copy(q).start()

    def finish(q):
        cols = span_f[q]

        @pl.when(moves)
        def _():
            first_copy(q).wait_recv()
            come(r2.at[:, :, cols], r2_r.at[q])

        @pl.when(stays)
        def _():
            come(r2.at[pl.ds(1, 3), :, cols], r2_r.at[q])
            first_in[:, cols] = first[:, cols]
            r2[0, :, cols] = s2[0, :, cols]

        second = r2[0, :, cols].astype(F32)
        for j in (1, 3, 2):
            second = second + r2[j, :, cols].astype(F32)
        result = coef_a * m_ref[:, cols].astype(F32) + coef_b * first_in[:, cols] + coef_c * second
        o_ref[:, cols] = result.astype(BF16)

    def product(q):
        cols = span_f[q]
        part = acc[:, cols] + jnp.dot(gt[:, early:], x_flat[early:, cols], preferred_element_type=F32)
        for j in (2, 1, 3):
            s1[j, :, cols] = part[j * ROWS:(j + 1) * ROWS].astype(BF16)
            y_copy(j, q).start()
        own[:, cols] = part[:ROWS]

    def second_product(q):
        cols = span_f[q]
        part = jnp.dot(gt[...], f_flat[:, cols], preferred_element_type=F32)
        for j in (2, 1, 3, 0):
            s2[j, :, cols] = part[j * ROWS:(j + 1) * ROWS].astype(BF16)
            if j > 0:
                last_copy(j, q).start()

        @pl.when(moves)
        def _():
            last_copy(0, q).start()

    def arrive(q, s):
        relay(f_copy, RIGHT_F, s, q)
        slots, start, rows = UNITS[s - 1]
        flatten([f_blk.at[(k - 1) % ZS] for k in slots], f_flat, start, rows, span_f[q])

    act = {
        "p": product, "s": start_ring, "h": hand_over, "r": arrive, "g": second_product,
        "f": finish,
    }
    for step in STEPS:
        act[step[0]](*map(int, step[1:]))

    @pl.when(moves)
    def _():
        sent(mz_blk.at[0], mz_s.at[0])
        sent(first, out_s)
        sent(s2.at[0], r2_s.at[0])

    three = pl.ds(0, 3)
    sent(mz_blk.at[three], mz_s.at[1])
    sent(x_blk, xz_s)
    sent(ex, ex_s)
    sent(gs.at[:, three], gr_s)
    sent(gs.at[:, three], gx_s)
    sent(gs, gc_s)
    sent(s1.at[three], r1_s)
    sent(f_blk.at[pl.ds(0, ZS - 1)], fz_s)
    sent(s2.at[three], r2_s.at[1])


def shards(momentum):
    vm, dma = pltpu.VMEM, pltpu.SemaphoreType.DMA
    blk = (ROWS, COLS)
    tile = (TILES, HEIGHT, LANE)
    scratch = [
        vm((YS,) + blk, BF16), vm((ZS - 1,) + blk, BF16), vm((ZS,) + blk, BF16),
        vm((HEIGHT, COLS), BF16), vm((DEPTH, COLS), BF16), vm((DEPTH, COLS), BF16),
        vm(tile, F32), vm(tile, F32), vm(tile, F32),
        vm((TILES, XS, ROWS, LANE), BF16), vm((TILES, XS - 1, ROWS, LANE), BF16),
        vm((XS, ROWS, DEPTH), BF16), vm((HEIGHT, DEPTH), BF16),
        vm((HEIGHT, COLS), F32), vm(blk, F32), vm(blk, F32), vm(blk, F32),
        vm((YS,) + blk, BF16), vm((YS,) + blk, BF16), vm((YS,) + blk, BF16), vm((YS,) + blk, BF16),
    ]
    nx, nf = len(RING_X), len(RING_F)
    for shape in (
        (2,), (nx + 2,), (), (5, nx), (), (5, nf), (), (2 * TILES,), (), (TILES,), (), (TILES,),
        (), (TILES,), (), (nf,), (2,), (nf,), (), (nf,),
    ):
        scratch.append(dma(shape))
    return pl.pallas_call(
        kernel,
        out_shape=jax.ShapeDtypeStruct(blk, BF16),
        in_specs=[pl.BlockSpec(memory_space=pltpu.VMEM)],
        out_specs=pl.BlockSpec(memory_space=pltpu.VMEM),
        scratch_shapes=scratch,
        compiler_params=pltpu.CompilerParams(
            collective_id=0, has_side_effects=True, vmem_limit_bytes=56 * 1024 * 1024
        ),
        name="newton_schulz",
    )(momentum)


def solution(mesh):
    in_specs = (P("row", "col"),)
    out_specs = P("row", "col")
    return jax.shard_map(shards, mesh=mesh, in_specs=in_specs, out_specs=out_specs, check_vma=False)
```

```python
import jax
import jax.numpy as jnp
from jax import lax
from jax.experimental import pallas as pl
from jax.experimental.pallas import tpu as pltpu
from jax.sharding import PartitionSpec as P

BREADTH = 9216
MESH = pl.DeviceIdType.MESH
F32 = jnp.float32
BF16 = jnp.bfloat16

coef_a = 3.4445
coef_b = -4.775
coef_c = 2.0315

ROWS, COLS = 168, 1152
ZS, YS, XS = 8, 4, 4
LANE = 128
RING_X = (1, 1, 2, 2, 3)
RING_F = (1, 1, 1, 1, 2, 2, 1)
RIGHT_X = (2, 3)
RIGHT_F = (0, 1, 2, 5)
STEPS = (
    "p0", "p1", "p2", "p3", "p4", "p5", "p6", "s0", "s1", "r01", "s2", "r11", "s3", "r02", "r21",
    "r12", "r31", "s4", "r03", "r22", "r13", "r32", "s5", "r41", "s6", "h0", "h1", "r23", "r04", "g0",
    "h2", "h3", "r33", "r14", "g1", "r51", "r42", "h4", "r61", "r24", "g2", "h5", "r52", "r34", "g3",
    "r43", "h6", "r62", "r53", "r44", "g4", "r63", "r54", "g5", "f0", "f1", "f2", "r64", "g6", "f3",
    "f4", "f5", "f6",
)
NEAR, FAR = (0, 1, 3), (2,)
UNITS = (((0, 1, 7), 0, 512), ((2, 6), 512, 384), ((3, 5), 896, 384), ((4,), 1280, 256))
DEPTH = 1536
HEIGHT = YS * ROWS
TILE = 2 * LANE
TILES = DEPTH // TILE


def chunks(widths):
    spans, start = [], 0
    for w in widths:
        spans.append(pl.ds(start * LANE, w * LANE))
        start += w
    return spans


def place(x, y, z, c):
    return (lax.rem(y, 2) * 16 + z * 2 + c, x * 2 + y // 2)


def flatten(blocks, dst, start, rows, cols):
    empty = rows - ROWS * len(blocks)
    for l in range(cols.start, cols.start + cols.size, LANE):
        parts = [blk[:, l:l + LANE].astype(F32) for blk in blocks]
        if empty:
            parts.append(jnp.zeros((empty, LANE), F32))
        stacked = parts[0] if len(parts) == 1 else jnp.concatenate(parts, axis=0)
        dst[start:start + rows, l:l + LANE] = stacked.astype(BF16)


def kernel(
    m_ref, o_ref,
    mz_blk, x_blk, f_blk, mz_flat, x_flat, f_flat,
    ex, er, gsum, gs, gr, gg, gt,
    acc, own, first, first_in, s1, r1, s2, r2,
    mz_s, mz_r, xz_s, xz_r, fz_s, fz_r,
    ex_s, ex_r, gr_s, gr_r, gx_s, gx_r, gc_s, gc_r,
    r1_s, r1_r, r2_s, r2_r, out_s, out_r,
):
    row, col = lax.axis_index("row"), lax.axis_index("col")
    x, y_hi = col // 2, lax.rem(col, 2)
    y_lo, z, c = row // 16, lax.rem(row // 2, ZS), lax.rem(row, 2)
    y = y_hi * 2 + y_lo

    def at_z(d):
        return place(x, y, lax.rem(z + d + ZS, ZS), c)

    def at_y(d):
        return place(x, lax.rem(y + d + YS, YS), z, c)

    def at_x(d):
        return place(lax.rem(x + d + XS, XS), y, z, c)

    other_core = place(x, y, z, 1 - c)
    home = c * 2 + y_lo

    def taker(j):
        return place(x, lax.rem(home - j + YS, YS), z, y_hi)

    partner = taker(0)

    def owner(j):
        to = lax.rem(y + j, YS)
        return place(x, c * 2 + lax.rem(to, 2), z, to // 2)

    stays = c == y_hi
    moves = jnp.logical_not(stays)

    def copy(src, dst, send, recv, to):
        return pltpu.make_async_remote_copy(
            src_ref=src, dst_ref=dst, send_sem=send, recv_sem=recv,
            device_id=to, device_id_type=MESH,
        )

    def sent(ref, sem):
        copy(ref, ref, sem, sem, other_core).wait_send()

    def come(ref, sem):
        copy(ref, ref, sem, sem, other_core).wait_recv()

    barrier = pltpu.get_barrier_semaphore()

    def greet(peer):
        pl.semaphore_signal(barrier, inc=1, device_id=peer, device_id_type=MESH)

    for peer in (
        [at_z(1), at_z(-1), other_core]
        + [at_y(d) for d in (1, 2, 3)] + [at_x(d) for d in (1, 2, 3)]
        + [taker(j) for j in (1, 2, 3)] + [owner(j) for j in (1, 2, 3)]
    ):
        greet(peer)

    @pl.when(moves)
    def _():
        greet(partner)
        pl.semaphore_wait(barrier, 16)

    @pl.when(stays)
    def _():
        pl.semaphore_wait(barrier, 15)

    span_x, span_f = chunks(RING_X), chunks(RING_F)
    nx, count = len(span_x), len(span_f)

    def mz_copy(j, q):
        where = mz_blk.at[j, :, span_x[q]]
        return copy(m_ref.at[:, span_x[q]], where, mz_s.at[min(j, 1)], mz_r.at[q if j == 0 else nx + (j == 2)], taker(j))

    @pl.when(stays)
    def _():
        mz_blk[0] = m_ref[...]

    @pl.when(moves)
    def _():
        for q in range(len(span_x)):
            mz_copy(0, q).start()

    def z_copy(own_blk, blk, spans, right, ss, rs, dst, q):
        if dst > 4 or (dst == 4 and q in right):
            src, to = (dst + 1) % ZS, at_z(1)
        else:
            src, to = dst - 1, at_z(-1)
        src_ref = own_blk.at[:, spans[q]] if src == 0 else blk.at[src - 1, :, spans[q]]
        return copy(src_ref, blk.at[dst - 1, :, spans[q]], ss, rs.at[min(dst, ZS - dst), q], to)

    def x_copy(dst, q):
        return z_copy(mz_blk.at[0], x_blk, span_x, RIGHT_X, xz_s, xz_r, dst, q)

    def f_copy(dst, q):
        return z_copy(f_blk.at[7], f_blk, span_f, RIGHT_F, fz_s, fz_r, dst, q)

    def relay(make, right, s, q):
        if s == 4:
            make(4, q).wait_recv()
            return
        blk, rs, spans = (x_blk, xz_r, span_x) if make is x_copy else (f_blk, fz_r, span_f)
        come(blk.at[pl.ds(0, 2), :, spans[q]], rs.at[s, q])
        for nxt, far in ((ZS - s - 1, q in right), (s + 1, q not in right)):
            if s < 3 or far:
                make(nxt, q).start()

    for q in range(len(span_x)):

        @pl.when(moves)
        def _():
            mz_copy(0, q).wait_recv()

        x_copy(7, q).start()
        x_copy(1, q).start()

    whole = pl.ds(0, COLS)

    def lanes(u, core):
        return pl.ds(pl.multiple_of((2 * u + core) * LANE, LANE), LANE)

    def ex_copy(u):
        return copy(ex.at[u], er.at[u], ex_s, ex_r.at[u], other_core)

    def gr_copy(u, d):
        p = lax.rem(x + d, XS)
        return copy(
            gs.at[u, p], gr.at[u, d - 1], gr_s, gr_r.at[u], at_x(d)
        )

    def gx_copy(u, d, p):
        where = gg.at[p, :, lanes(u, c)]
        return copy(where, where, gx_s, gx_r.at[u], at_x(d))

    def gc_copy(u, core):
        where = gg.at[:, :, lanes(u, core)]
        return copy(where, where, gc_s, gc_r.at[u], other_core)

    def flatten_x(s):
        slots, start, rows = UNITS[s - 1]
        blocks = [mz_blk.at[0] if k == 0 else x_blk.at[k - 1] for k in slots]
        flatten(blocks, x_flat, start, rows, whole)

    def relay_one(s, q):
        relay(x_copy, RIGHT_X, s, q)

    def stage_a(u):
        part = lax.dot_general(
            mz_flat[...], x_flat[u * TILE:(u + 1) * TILE, :], (((1,), (1,)), ((), ())),
            preferred_element_type=F32,
        )
        part = part * (1.0 / BREADTH)
        ex[u] = jnp.where(c == 0, part[:, LANE:], part[:, :LANE])
        ex_copy(u).start()
        gsum[u] = jnp.where(c == 0, part[:, :LANE], part[:, LANE:])

    def block_rows(j):
        return slice(j * ROWS, (j + 1) * ROWS)

    def part_copy(u, rows, far):
        return copy(ex.at[u, rows], er.at[u, rows], ex_s, ex_r.at[far * TILES + u], other_core)

    def parts_a(u, js, sends):
        for j in js:
            part = lax.dot_general(
                mz_blk[j], x_flat[u * TILE:(u + 1) * TILE, :], (((1,), (1,)), ((), ())),
                preferred_element_type=F32,
            )
            part = part * (1.0 / BREADTH)
            ex[u, block_rows(j), :] = jnp.where(c == 0, part[:, LANE:], part[:, :LANE])
            gsum[u, block_rows(j), :] = jnp.where(c == 0, part[:, :LANE], part[:, LANE:])
        for rows in sends:
            part_copy(u, rows, js == FAR).start()

    def parts_b(u, js):
        some = pl.ds(0, ROWS * len(js))
        come(er.at[u, some], ex_r.at[(js == FAR) * TILES + u])
        for j in js:
            total = gsum[u, block_rows(j), :] + er[u, block_rows(j), :]
            gsum[u, block_rows(j), :] = total
            gs[u, j] = total.astype(BF16)

            @pl.when(x != j)
            def _():
                slot = lax.rem(j - x + XS, XS) - 1
                copy(gs.at[u, j], gr.at[u, slot], gr_s, gr_r.at[u], place(j, y, z, c)).start()

    def parts_c(u, js):
        ours = x == 2 if js == FAR else x != 2

        @pl.when(ours)
        def _():
            stage_c(u)

    def near_a(u):
        parts_a(u, NEAR, (pl.ds(0, 2 * ROWS), pl.ds(3 * ROWS, ROWS)))

    def far_a(u):
        parts_a(u, FAR, (pl.ds(2 * ROWS, ROWS),))

    def stage_b(u):
        ex_copy(u).wait_recv()
        total = gsum[u] + er[u]
        gsum[u] = total
        for p in range(XS):
            gs[u, p] = total[p * ROWS:(p + 1) * ROWS].astype(BF16)
        for d in (1, 3, 2):
            gr_copy(u, d).start()

    def stage_c(u):
        come(gr.at[u], gr_r.at[u])
        total = gsum[u, pl.ds(pl.multiple_of(x * ROWS, 8), ROWS), :]
        for d in range(3):
            total = total + gr[u, d].astype(F32)
        gg[x, :, lanes(u, c)] = total.astype(BF16)
        for d in (1, 3, 2):
            gx_copy(u, d, x).start()

    def stage_d(u):
        come(gr.at[u], gx_r.at[u])
        gc_copy(u, c).start()

    def stage_e(u):
        gc_copy(u, 1 - c).wait_recv()
        flatten([gg.at[p] for p in range(XS)], gt, 0, HEIGHT, pl.ds(u * TILE, TILE))

    for q in range(nx):
        relay_one(1, q)
        if q == 1:
            for i in range(nx):
                for j in (1, 3):
                    mz_copy(j, i).start()
    flatten_x(1)
    come(mz_blk.at[pl.ds(1, 2)], mz_r.at[nx])
    for i in range(nx):
        mz_copy(2, i).start()
    near_a(0)
    relay_one(2, 0)
    near_a(1)
    relay_one(2, 1)
    parts_b(0, NEAR)
    parts_b(1, NEAR)
    relay_one(2, 2)
    relay_one(2, 3)
    come(mz_blk.at[2], mz_r.at[nx + 1])
    far_a(0)
    far_a(1)
    flatten([mz_blk.at[j] for j in range(YS)], mz_flat, 0, HEIGHT, whole)
    parts_c(0, NEAR)
    relay_one(2, 4)
    flatten_x(2)
    stage_a(2)
    parts_b(0, FAR)
    parts_b(1, FAR)
    parts_c(1, NEAR)
    relay_one(3, 0)
    relay_one(3, 1)
    stage_b(2)
    relay_one(3, 2)
    relay_one(3, 3)
    relay_one(3, 4)
    flatten_x(3)
    stage_a(3)
    stage_a(4)
    parts_c(0, FAR)
    parts_c(1, FAR)
    stage_b(3)
    stage_b(4)
    stage_c(2)
    stage_d(0)
    stage_d(1)
    for q in range(nx):
        relay_one(4, q)
    flatten_x(4)
    stage_a(5)
    stage_c(3)
    stage_b(5)
    stage_d(2)
    stage_c(4)
    stage_e(0)
    stage_e(1)
    stage_d(3)
    stage_c(5)
    stage_e(2)
    stage_d(4)
    stage_e(3)
    stage_d(5)
    early = 4 * TILE
    acc[...] = jnp.dot(gt[:, :early], x_flat[:early, :], preferred_element_type=F32)
    stage_e(4)
    stage_e(5)

    def y_copy(j, q):
        where = (j, slice(None), span_f[q])
        return copy(s1.at[where], r1.at[where], r1_s, r1_r.at[q], at_y(j))

    def last_copy(j, q):
        where = (j, slice(None), span_f[q])
        return copy(s2.at[where], r2.at[where], r2_s.at[min(j, 1)], r2_r.at[q], owner(j))

    def start_ring(q):
        cols = span_f[q]
        total = own[:, cols]
        come(r1.at[pl.ds(1, 3), :, cols], r1_r.at[q])
        for j in (1, 3, 2):
            total = total + r1[j, :, cols].astype(F32)
        first[:, cols] = total
        f_blk[7, :, cols] = total.astype(BF16)
        f_copy(7, q).start()
        f_copy(1, q).start()

    def first_copy(q):
        where = (slice(None), span_f[q])
        return copy(first.at[where], first_in.at[where], out_s, out_r.at[q], partner)

    def hand_over(q):
        @pl.when(moves)
        def _():
            first_copy(q).start()

    def finish(q):
        cols = span_f[q]

        @pl.when(moves)
        def _():
            first_copy(q).wait_recv()
            come(r2.at[:, :, cols], r2_r.at[q])

        @pl.when(stays)
        def _():
            come(r2.at[pl.ds(1, 3), :, cols], r2_r.at[q])
            first_in[:, cols] = first[:, cols]
            r2[0, :, cols] = s2[0, :, cols]

        second = r2[0, :, cols].astype(F32)
        for j in (1, 3, 2):
            second = second + r2[j, :, cols].astype(F32)
        result = coef_a * m_ref[:, cols].astype(F32) + coef_b * first_in[:, cols] + coef_c * second
        o_ref[:, cols] = result.astype(BF16)

    def product(q):
        cols = span_f[q]
        part = acc[:, cols] + jnp.dot(gt[:, early:], x_flat[early:, cols], preferred_element_type=F32)
        for j in (2, 1, 3):
            s1[j, :, cols] = part[j * ROWS:(j + 1) * ROWS].astype(BF16)
            y_copy(j, q).start()
        own[:, cols] = part[:ROWS]

    def second_product(q):
        cols = span_f[q]
        part = jnp.dot(gt[...], f_flat[:, cols], preferred_element_type=F32)
        for j in (2, 1, 3, 0):
            s2[j, :, cols] = part[j * ROWS:(j + 1) * ROWS].astype(BF16)
            if j > 0:
                last_copy(j, q).start()

        @pl.when(moves)
        def _():
            last_copy(0, q).start()

    def arrive(q, s):
        relay(f_copy, RIGHT_F, s, q)
        slots, start, rows = UNITS[s - 1]
        flatten([f_blk.at[(k - 1) % ZS] for k in slots], f_flat, start, rows, span_f[q])

    act = {
        "p": product, "s": start_ring, "h": hand_over, "r": arrive, "g": second_product,
        "f": finish,
    }
    for step in STEPS:
        act[step[0]](*map(int, step[1:]))

    @pl.when(moves)
    def _():
        sent(mz_blk.at[0], mz_s.at[0])
        sent(first, out_s)
        sent(s2.at[0], r2_s.at[0])

    three = pl.ds(0, 3)
    sent(mz_blk.at[three], mz_s.at[1])
    sent(x_blk, xz_s)
    sent(ex, ex_s)
    sent(gs.at[:, three], gr_s)
    sent(gs.at[:, three], gx_s)
    sent(gs, gc_s)
    sent(s1.at[three], r1_s)
    sent(f_blk.at[pl.ds(0, ZS - 1)], fz_s)
    sent(s2.at[three], r2_s.at[1])


def shards(momentum):
    vm, dma = pltpu.VMEM, pltpu.SemaphoreType.DMA
    blk = (ROWS, COLS)
    tile = (TILES, HEIGHT, LANE)
    scratch = [
        vm((YS,) + blk, BF16), vm((ZS - 1,) + blk, BF16), vm((ZS,) + blk, BF16),
        vm((HEIGHT, COLS), BF16), vm((DEPTH, COLS), BF16), vm((DEPTH, COLS), BF16),
        vm(tile, F32), vm(tile, F32), vm(tile, F32),
        vm((TILES, XS, ROWS, LANE), BF16), vm((TILES, XS - 1, ROWS, LANE), BF16),
        vm((XS, ROWS, DEPTH), BF16), vm((HEIGHT, DEPTH), BF16),
        vm((HEIGHT, COLS), F32), vm(blk, F32), vm(blk, F32), vm(blk, F32),
        vm((YS,) + blk, BF16), vm((YS,) + blk, BF16), vm((YS,) + blk, BF16), vm((YS,) + blk, BF16),
    ]
    nx, nf = len(RING_X), len(RING_F)
    for shape in (
        (2,), (nx + 2,), (), (5, nx), (), (5, nf), (), (2 * TILES,), (), (TILES,), (), (TILES,),
        (), (TILES,), (), (nf,), (2,), (nf,), (), (nf,),
    ):
        scratch.append(dma(shape))
    return pl.pallas_call(
        kernel,
        out_shape=jax.ShapeDtypeStruct(blk, BF16),
        in_specs=[pl.BlockSpec(memory_space=pltpu.VMEM)],
        out_specs=pl.BlockSpec(memory_space=pltpu.VMEM),
        scratch_shapes=scratch,
        compiler_params=pltpu.CompilerParams(
            collective_id=0, has_side_effects=True, vmem_limit_bytes=56 * 1024 * 1024
        ),
        name="newton_schulz",
    )(momentum)


def solution(mesh):
    in_specs = (P("row", "col"),)
    out_specs = P("row", "col")
    return jax.shard_map(shards, mesh=mesh, in_specs=in_specs, out_specs=out_specs, check_vma=False)
```
